256 devices in a mesh: vocab: 32 (over y, x, core), width: 8 (over z).
Axes of the slice: x: 4, y: 4, z: 8, core: 2. Of those that a mesh axis runs over, the one named last changes fastest.
Arguments:
- hidden: bfloat16 [512, 5376], P(None, 'width'), may hold values from -3 to 3
- weight: float32 [32768, 5376], P('vocab', 'width'), may hold values from -1.1 to 1.1, as said below
- scale: float32 [32768], P('vocab'), may hold values from 0.01 to 0.1
- flags: int32 [32768], P('vocab'), may hold values from 0 to 1
- targets: int32 [512], replicated, may hold values from 0 to 32767, as said below
Outputs:
- grad_weight: float32 [32768, 5376], P('vocab', 'width')
- grad_scale: float32 [32768], P('vocab')
- grad_hidden: float32 [512, 5376], P(None, 'width')
- loss: float32 [], replicated
The draws below stay inside these ranges and needn't reach their ends.
Inputs may be any that keep to these rules, and one draw needn't show every extreme that they name: `targets`: no target is a padded row. weight / scale stays 0.1 or more away from every odd multiple of 0.5.
All inputs are finite; a program needn't handle non-finite values.
Results may differ from the reference program's by a relative error of at most 0.0009.
The reference program's roundings to bfloat16 on the way (of `quantized` and `dlogits`) count: a program that leaves them out, or rounds other values in their place, can miss the bound.
Values may be sent and summed in bfloat16 or wider, within the bound.
A program may use at most 64 MiB of HBM per device.

```python
import math
import jax
import jax.numpy as jnp
from jax import lax

D = 5376
TOKENS = 512
VOCAB = 32768


def padding(key):
    flag_key = jax.random.fold_in(key, 101)
    return (jax.random.randint(flag_key, (VOCAB,), 0, 8) == 0).astype(jnp.int32)


def quant_parts(key):
    part_key = jax.random.fold_in(key, 303)
    key_one, key_two, key_three, key_four, key_five = jax.random.split(part_key, 5)
    spans = jax.random.randint(key_four, (VOCAB,), 1, 8)
    amplitudes = jnp.exp(jax.random.uniform(key_one, (VOCAB,), jnp.float32, math.log(0.07), math.log(0.1)))
    steps = amplitudes / spans.astype(jnp.float32)
    offsets = jax.random.randint(key_five, (D,), -1, 2)
    noise = jax.random.randint(key_two, (VOCAB, D), -spans[:, None], spans[:, None] + 1)
    levels = (spans[:, None] * offsets[None, :] + noise).astype(jnp.float32)
    fraction = jax.random.uniform(key_three, (VOCAB, D), jnp.float32, -0.4, 0.4)
    return (steps, levels, fraction)


def draw_flags(key, part):
    return padding(key)


def draw_targets(key, part):
    flags = padding(key)
    own_key = jax.random.fold_in(key, 2)
    order = jnp.argsort(flags, stable=True).astype(jnp.int32)
    usable_count = VOCAB - jnp.sum(flags)
    chosen = jax.random.randint(own_key, (TOKENS,), 0, usable_count)
    return order[chosen].astype(jnp.int32)


def draw_scale(key, part):
    steps, levels, fraction = quant_parts(key)
    return steps


def draw_weight(key, part):
    steps, levels, fraction = quant_parts(key)
    return steps[:, None] * (levels + fraction)


def draw_hidden(key, part):
    own_key = jax.random.fold_in(key, 505)
    key_one = jax.random.fold_in(own_key, 0)
    limit = float(max(3, 3072 // D))
    values = 0.55 * jnp.clip(jax.random.normal(key_one, (TOKENS, D), jnp.float32), -6.0, 6.0)
    return jnp.clip(values, -limit, limit).astype(jnp.bfloat16)


def setup_inputs(seed: int = 0) -> dict:
    seeds = jax.random.split(jax.random.key(seed), 6)
    return {
        "hidden": draw_hidden(jax.random.fold_in(seeds[5], 71), 0),
        "weight": draw_weight(jax.random.fold_in(seeds[5], 71), 0),
        "scale": draw_scale(jax.random.fold_in(seeds[5], 71), 0),
        "flags": draw_flags(jax.random.fold_in(seeds[5], 71), 0),
        "targets": draw_targets(jax.random.fold_in(seeds[5], 71), 0),
    }


def reference(hidden, weight, scale, flags, targets):
    ratios = weight / scale[:, None]
    rounded = jnp.floor(ratios + 0.5)
    levels = jnp.clip(rounded, -8.0, 7.0)
    inside = ((rounded >= -8.0) & (rounded <= 7.0)).astype(jnp.float32)
    quantized = (scale[:, None] * levels).astype(jnp.bfloat16)
    logits = jnp.dot(hidden, quantized.T, preferred_element_type=jnp.float32)
    usable = flags == 0
    masked = jnp.where(usable[None, :], logits, -1e+30)
    row_top = lax.optimization_barrier(jnp.max(masked, axis=1))
    exp_terms = jnp.where(usable[None, :], jnp.exp(logits - row_top[:, None]), 0.0)
    row_total = lax.optimization_barrier(jnp.sum(exp_terms, axis=1))
    onehot = jnp.arange(logits.shape[1], dtype=jnp.int32)[None, :] == targets[:, None]
    picked = lax.optimization_barrier(jnp.sum(jnp.where(onehot, logits, 0.0), axis=1))
    loss = jnp.sum(row_top + jnp.log(row_total) - picked)
    dlogits = (exp_terms / row_total[:, None] - onehot.astype(jnp.float32)).astype(jnp.bfloat16)
    dquant = jnp.dot(dlogits.T, hidden, preferred_element_type=jnp.float32)
    grad_hidden = jnp.dot(dlogits, quantized, preferred_element_type=jnp.float32)
    grad_weight = inside * dquant + 0.1 * usable.astype(jnp.float32)[:, None] * weight
    scale_terms = lax.optimization_barrier(jnp.sum(dquant * (levels - inside * ratios), axis=1))
    grad_scale = scale_terms * (1.0 / math.sqrt(D * 7.0))
    return (grad_weight, grad_scale, grad_hidden, loss)
```

```python
import functools
import math

import jax
import jax.numpy as jnp
from jax import lax
from jax.experimental import pallas as pl
from jax.experimental.pallas import tpu as pltpu
from jax.sharding import PartitionSpec as P

D = 5376
NEG_FILL = -1e30
DECAY = 0.1
MESH = pl.DeviceIdType.MESH

NZ = 8
NG = 8
NY = 4
TB = 64
NS = 4
HB = TB // NS
ROWS = 1024
COLS = 672
PAD = 768
FOLD = 384

CODE_TOP = 32000.0
UNIT = math.log(2.0) / 256.0
ROOT_TOP = 65535.0
ROOT_MID = 32768.0


def code_step(x, top_code, axis):
    top = jnp.max(jnp.abs(x), axis=axis, keepdims=True)
    e = jnp.ceil(jnp.log(jnp.maximum(top, 1e-30) * (1.0 / top_code)) * (1.0 / UNIT))
    return e, jnp.exp(e * (-UNIT))


def to_codes(x, inv):
    return jnp.floor(x * inv + 0.5)


def kernel(
    hid_hbm, w_hbm, sc_hbm, fl_hbm, tg_hbm,
    gw_out, gs_out, gh_out, loss_out,
    w_v, sc1, fl1, tg4, ht_s, q_s, h_s, part, dl_s, tr_s, zt_s, own_s, root_s,
    rs_out, rs_in, ag_s, st_a, st_b, st_z, gh_s, a_out, a_in, b_buf, c_buf, f_buf,
    w_sem, h_sem, small_sem,
    rs_send, rs_recv, ag_send, ag_recv,
    sa_send, sa_recv, sb_send, sb_recv, sz_send, sz_recv,
    a_send, a_recv, b_send, b_recv, c_send, c_recv, f_send, f_recv,
):
    f32, bf16, i32, i16 = jnp.float32, jnp.bfloat16, jnp.int32, jnp.int16
    v = lax.axis_index("vocab")
    w = lax.axis_index("width")
    core = lax.rem(v, 2)
    x = lax.rem(lax.div(v, 2), 4)
    y = lax.div(v, 8)
    right = (v, lax.rem(w + 1, NZ))
    left = (v, lax.rem(w + NZ - 1, NZ))

    def g_index(mode):
        return (x if mode == "x" else y) * 2 + core

    def g_peer(mode, j):
        other = lax.rem(g_index(mode) + j, NG)
        far, far_core = lax.div(other, 2), lax.rem(other, 2)
        if mode == "x":
            return other, ((y * 4 + far) * 2 + far_core, w)
        return other, ((far * 4 + x) * 2 + far_core, w)

    def y_index(mode):
        return y if mode == "x" else x

    def y_peer(mode, j):
        other = lax.rem(y_index(mode) + j, NY)
        if mode == "x":
            return other, ((other * 4 + x) * 2 + core, w)
        return other, ((y * 4 + other) * 2 + core, w)

    def z_peer(j):
        return (v, lax.rem(w + j, NZ))

    def block_rows(shift, half=None):
        block = lax.rem(w + (shift + 2 * NZ), NZ)
        if half is None:
            return pl.ds(pl.multiple_of(block * TB, TB), TB)
        return pl.ds(pl.multiple_of(block * TB + half * HB, HB), HB)

    small_copies = [
        pltpu.make_async_copy(src, dst, small_sem.at[i])
        for i, (src, dst) in enumerate([(tg_hbm, tg4), (sc_hbm, sc1), (fl_hbm, fl1)])
    ]
    for copy in small_copies:
        copy.start()
    WB = 256

    def w_copy(i):
        cols = pl.ds(pl.multiple_of(i * WB, WB), WB)
        return pltpu.make_async_copy(w_hbm.at[:, cols], w_v.at[:, cols], w_sem.at[i])

    @pl.loop(0, ROWS // WB)
    def _(i):
        w_copy(i).start()

    h_copy = pltpu.make_async_copy(hid_hbm, ht_s.at[pl.ds(0, COLS)], h_sem)
    h_copy.start()

    barrier = pltpu.get_barrier_semaphore()
    for j in range(1, NZ):
        pl.semaphore_signal(barrier, inc=1, device_id=z_peer(j), device_id_type=MESH)
    for j in range(1, NG):
        pl.semaphore_signal(
            barrier, inc=1, device_id=g_peer("x", j)[1], device_id_type=MESH
        )
    for j in range(2, NG):
        far = lax.rem(y + lax.div(j, 2), 4)
        pl.semaphore_signal(
            barrier,
            inc=1,
            device_id=((far * 4 + x) * 2 + j % 2, w),
            device_id_type=MESH,
        )

    for copy in small_copies:
        copy.wait()
    tr_s[...] = jnp.transpose(
        jnp.concatenate([tg4[...].astype(f32), jnp.zeros((124, 128), f32)], axis=0)
    )
    ht_s[COLS:, :] = jnp.zeros((PAD - COLS, 512), bf16)
    q_s[COLS:, :] = jnp.zeros((PAD - COLS, ROWS), bf16)
    h_copy.wait()

    @pl.loop(0, ROWS // WB)
    def _(i):
        w_copy(i).wait()
        tokens = pl.ds(pl.multiple_of(i * 128, 128), 128)
        h_s[tokens, :] = jnp.transpose(ht_s[:, tokens])
        cols = pl.ds(pl.multiple_of(i * WB, WB), WB)
        scale = sc1[:, cols]
        rounded = jnp.floor(w_v[:, cols] * (1.0 / scale) + 0.5)
        levels = jnp.clip(rounded, -8.0, 7.0)
        q_s[:COLS, cols] = (scale * levels).astype(bf16)

    def logits_of(shifts):
        rows = [h_s[block_rows(shift), :] for shift in shifts]
        values = jnp.dot(
            jnp.concatenate(rows, axis=0) if len(shifts) > 1 else rows[0],
            q_s[...],
            preferred_element_type=f32,
        )
        for i, shift in enumerate(shifts):
            part[block_rows(shift), :] = values[i * TB : (i + 1) * TB, :]

    logits_of((4,))
    pl.semaphore_wait(barrier, (NZ - 1) + (NG - 1) + (NG - 2))

    lane_half = lax.broadcasted_iota(i32, (HB, 128), 1)

    def rs_copy(way, step, half):
        return pltpu.make_async_remote_copy(
            src_ref=rs_out.at[way, step, half],
            dst_ref=rs_in.at[way, step, half],
            send_sem=rs_send.at[way, step, half],
            recv_sem=rs_recv.at[way, step, half],
            device_id=right if way == 0 else left,
            device_id_type=MESH,
        )

    def encode(value, ref):
        e, inv = code_step(value, 4.0 * CODE_TOP, 1)
        codes = to_codes(value, inv).astype(i32)
        ref[:, :ROWS] = (codes >> 2).astype(i16)
        low = codes & 3
        pairs = low[:, :128]
        for i in range(1, ROWS // 128):
            pairs = pairs | (low[:, i * 128 : (i + 1) * 128] << (2 * i))
        ref[:, ROWS:] = jnp.where(lane_half == 0, e.astype(i32), pairs).astype(i16)

    def decode(ref):
        high = ref[:, :ROWS].astype(i32) << 2
        pairs = ref[:, ROWS:].astype(i32)
        unit = jnp.exp(pairs[:, :1].astype(f32) * UNIT)
        blocks = []
        for i in range(ROWS // 128):
            low = jnp.where(lane_half == 0, 1.5, ((pairs >> (2 * i)) & 3).astype(f32))
            blocks.append(high[:, i * 128 : (i + 1) * 128].astype(f32) + low)
        return jnp.concatenate(blocks, axis=1) * unit

    def rs_get(way, step, sub):
        return decode(rs_in.at[way, step, sub])

    def mine(shift, half):
        return part[block_rows(shift, half), :]

    firsts = ([s for s in range(NS) if s < NS // 2], [s for s in range(NS) if s >= NS // 2])

    def rs_pair(n, add):
        step = lax.div(n, NS)
        subs = (lax.rem(n + NS // 2, NS), lax.rem(n, NS))
        if add:
            for way in (0, 1):
                rs_copy(way, step - 1, subs[way]).wait_recv()
        values = [mine(4 - step, subs[0]), mine(step - 4, subs[1])]
        if add:
            values = [values[way] + rs_get(way, step - 1, subs[way]) for way in (0, 1)]
        for way in (0, 1):
            encode(values[way], rs_out.at[way, step, subs[way]])
        for way in (0, 1):
            rs_copy(way, step, subs[way]).start()

    @pl.loop(NS // 2, NS)
    def _(n):
        rs_pair(n, False)

    logits_of((3, -3))

    @pl.loop(NS, NS + NS // 2)
    def _(n):
        rs_pair(n, False)

    logits_of((2, -2))

    @pl.loop(NS + NS // 2, 2 * NS)
    def _(n):
        rs_pair(n, True)

    logits_of((1, -1, 0))

    @pl.loop(2 * NS, 4 * NS)
    def _(n):
        rs_pair(n, True)

    def ag_ref(way, step, sub):
        block = lax.rem(w + (step if way == 1 else NZ - step), NZ)
        return ag_s.at[block, sub]

    def ag_copy(way, step, sub):
        ref = ag_ref(way, step, sub)
        return pltpu.make_async_remote_copy(
            src_ref=ref,
            dst_ref=ref,
            send_sem=ag_send.at[way, step, sub],
            recv_sem=ag_recv.at[way, step, sub],
            device_id=right if way == 0 else left,
            device_id_type=MESH,
        )

    def ag_wait(way, step, sub):
        ref = ag_ref(way, step + 1, sub)
        pltpu.make_async_copy(ref, ref, ag_recv.at[way, step, sub]).wait()

    def ag_step(step):
        for sub in range(NS):
            for way in (0, 1):
                ag_wait(way, step, sub)
                if sub in firsts[way]:
                    ag_copy(way, step + 1, sub).start()
                else:

                    @pl.when(step < 2)
                    def _():
                        ag_copy(way, step + 1, sub).start()

    def ag_last():
        for way in (0, 1):
            for sub in firsts[way]:
                ag_wait(way, 3, sub)

    usable_row = fl1[...] == 0

    def pick_lane(ref, index, rows):
        at = lax.broadcasted_iota(i32, (rows.size, 128), 1)
        return jnp.sum(jnp.where(at == index, ref[rows, :], 0.0), axis=1, keepdims=True)

    def hits(block, first, count):
        rows = pl.ds(pl.multiple_of(lax.rem(block, 2) * TB + first, count), count)
        column = pick_lane(tr_s, lax.div(block, 2), rows).astype(i32) - v * ROWS
        return lax.broadcasted_iota(i32, (count, ROWS), 1) == column

    @pl.loop(0, NS)
    def _(sub):
        for way in (0, 1):
            rs_copy(way, 3, sub).wait_recv()
        own = mine(0, sub) + rs_get(0, 3, sub) + rs_get(1, 3, sub)
        masked = jnp.where(usable_row, own, NEG_FILL)
        top = jnp.max(masked, axis=1, keepdims=True)
        root = jnp.where(usable_row, jnp.exp((masked - top) * 0.5), 0.0)
        codes = jnp.floor(root * ROOT_TOP + (0.5 - ROOT_MID))
        ag_s[w, sub] = codes.astype(i32).astype(i16)
        for way in (0, 1):
            ag_copy(way, 0, sub).start()
        rows = pl.ds(pl.multiple_of(sub * HB, HB), HB)
        part[block_rows(0, sub), :] = own
        root_s[rows, :] = root
        own_s[rows, :] = jnp.broadcast_to(top, (HB, 128))

    lane = lax.broadcasted_iota(i32, (TB, 128), 1)
    total = jnp.sum(root_s[...] * root_s[...], axis=1, keepdims=True)
    picked = jnp.sum(
        jnp.where(hits(w, 0, TB), part[block_rows(0), :], 0.0), axis=1, keepdims=True
    )
    stats = jnp.where(
        lane == 0,
        own_s[...],
        jnp.where(lane == 1, total, jnp.where(lane == 2, picked, 0.0)),
    )

    stats = jnp.transpose(jnp.concatenate([stats, jnp.zeros((TB, 128), f32)], axis=0))
    g = g_index("x")
    st_a[g] = stats[:8, :]
    for j in range(1, NG):
        pltpu.make_async_remote_copy(
            src_ref=st_a.at[g], dst_ref=st_a.at[g], send_sem=sa_send, recv_sem=sa_recv,
            device_id=g_peer("x", j)[1], device_id_type=MESH,
        ).start()

    def wait_bytes(ref, sem):
        pltpu.make_async_copy(ref, ref, sem).wait()

    def merge(buf, n):
        best = buf[0, 0:1, :]
        for i in range(1, n):
            best = jnp.maximum(best, buf[i, 0:1, :])
        weight = jnp.zeros((1, 128), f32)
        pick = jnp.zeros((1, 128), f32)
        for i in range(n):
            weight += buf[i, 1:2, :] * jnp.exp(buf[i, 0:1, :] - best)
            pick += buf[i, 2:3, :]
        return best, weight, pick

    @pl.loop(0, 3)
    def _(step):
        ag_step(step)

        @pl.when(step == 0)
        def _():
            wait_bytes(st_a.at[pl.ds(0, NG - 1)], sa_recv)
            best, weight, pick = merge(st_a, NG)
            st_b[y] = jnp.concatenate([best, weight, pick, jnp.zeros((5, 128), f32)], axis=0)
            for j in range(1, NY):
                pltpu.make_async_remote_copy(
                    src_ref=st_b.at[y], dst_ref=st_b.at[y], send_sem=sb_send, recv_sem=sb_recv,
                    device_id=y_peer("x", j)[1], device_id_type=MESH,
                ).start()

        @pl.when(step == 1)
        def _():
            wait_bytes(st_b.at[pl.ds(0, NY - 1)], sb_recv)
            best, weight, pick = merge(st_b, NY)
            lane_row = lax.broadcasted_iota(i32, (1, 128), 1)
            loss_row = jnp.where(lane_row < TB, best + jnp.log(weight) - pick, 0.0)
            f_buf[w, pl.ds(8, 8), :] = jnp.broadcast_to(loss_row, (8, 128))
            factor = jnp.exp(st_a[g, 0:1, :] - best) / weight
            st_z[w] = jnp.broadcast_to(factor * (1.0 / (ROOT_TOP * ROOT_TOP)), (8, 128))
            for j in range(1, NZ):
                pltpu.make_async_remote_copy(
                    src_ref=st_z.at[w], dst_ref=st_z.at[w], send_sem=sz_send, recv_sem=sz_recv,
                    device_id=z_peer(j), device_id_type=MESH,
                ).start()

    wait_bytes(st_z.at[pl.ds(0, NZ - 1)], sz_recv)
    rows_of = [st_z[i, 0:1, :] for i in range(NZ)]
    zt_s[...] = jnp.transpose(
        jnp.concatenate(rows_of + [jnp.zeros((120, 128), f32)], axis=0)
    )

    def form_dlogits(shift):
        block = lax.rem(w + (shift + NZ), NZ)
        factor = pick_lane(zt_s, block, pl.ds(0, TB))
        codes = jnp.concatenate([ag_s[block, s] for s in range(NS)], axis=0)
        root = codes.astype(i32).astype(f32) + ROOT_MID
        dl_s[block_rows(shift), :] = (
            root * root * factor - hits(block, 0, TB).astype(f32)
        ).astype(bf16)

    groups = [(-1, 0, 1), (-2, 2), (-3, 3), (4,)]
    modes = ["x", "y", "y", "x"]
    nt = (((1,), (1,)), ((), ()))

    def fold(x):
        n = x.shape[0] // 8
        e, inv = code_step(x, CODE_TOP, 1)
        wide = lax.broadcasted_iota(i32, (8 * n, PAD), 1)
        codes = jnp.where(wide < COLS, to_codes(x, inv), e).astype(i32)
        return jnp.concatenate(
            [codes[:, :FOLD].reshape(n, 8, FOLD), codes[:, FOLD:].reshape(n, 8, FOLD)], axis=1
        ).astype(i16)

    def unfold(piece):
        n = piece.shape[0]
        codes = piece.astype(i32).astype(f32)
        low = codes[:, :8, :].reshape(8 * n, FOLD)
        high = codes[:, 8:, :].reshape(8 * n, FOLD)
        unit = jnp.exp(high[:, FOLD - 1 :] * UNIT)
        wide = jnp.concatenate([low, high], axis=1)
        lane_pad = lax.broadcasted_iota(i32, (8 * n, PAD), 1)
        return jnp.where(lane_pad < COLS, wide * unit, 0.0)

    def stage_a(k):
        n = len(groups[k])
        terms = [dl_s[block_rows(shift), :] for shift in groups[k]]
        term = lax.dot_general(
            jnp.concatenate(terms, axis=0) if n > 1 else terms[0],
            q_s[...],
            nt,
            preferred_element_type=f32,
        )
        g = g_index(modes[k])
        for s in range(n):
            a_out[k, :, s] = fold(term[s * TB : (s + 1) * TB])
        a_in[k, g] = a_out[k, g]
        for j in range(1, NG):
            other, device = g_peer(modes[k], j)
            pltpu.make_async_remote_copy(
                src_ref=a_out.at[k, other, pl.ds(0, n)], dst_ref=a_in.at[k, g, pl.ds(0, n)],
                send_sem=a_send.at[k], recv_sem=a_recv.at[k],
                device_id=device, device_id_type=MESH,
            ).start()

    def stage_b(k):
        n = len(groups[k])
        wait_bytes(a_in.at[k, pl.ds(0, NG - 1), pl.ds(0, n)], a_recv.at[k])
        total = unfold(a_in[k, 0, :n])
        for i in range(1, NG):
            total += unfold(a_in[k, i, :n])
        at = y_index(modes[k])
        b_buf[k, at, :n] = fold(total)
        for j in range(1, NY):
            mine_ref = b_buf.at[k, at, pl.ds(0, n)]
            pltpu.make_async_remote_copy(
                src_ref=mine_ref, dst_ref=mine_ref,
                send_sem=b_send.at[k], recv_sem=b_recv.at[k],
                device_id=y_peer(modes[k], j)[1], device_id_type=MESH,
            ).start()

    def stage_c(k):
        n = len(groups[k])
        wait_bytes(b_buf.at[k, pl.ds(0, NY - 1), pl.ds(0, n)], b_recv.at[k])
        total = unfold(b_buf[k, 0, :n])
        for i in range(1, NY):
            total += unfold(b_buf[k, i, :n])
        g = g_index(modes[k])
        c_buf[k, g, :n] = fold(total)
        for j in range(1, NG):
            mine_ref = c_buf.at[k, g, pl.ds(0, n)]
            pltpu.make_async_remote_copy(
                src_ref=mine_ref, dst_ref=mine_ref,
                send_sem=c_send.at[k], recv_sem=c_recv.at[k],
                device_id=g_peer(modes[k], j)[1], device_id_type=MESH,
            ).start()

    odd = lax.rem(w, 2)
    unit_blocks = [w, w + 2 * odd - 1, w + 2 - 4 * odd, w + 4]

    def unit_lanes(k):
        unit = lax.div(lax.rem(unit_blocks[k] + NZ, NZ), 2)
        return pl.ds(pl.multiple_of(unit * 128, 128), 128)

    def stage_d(k):
        n = len(groups[k])
        wait_bytes(c_buf.at[k, pl.ds(0, NG - 1), pl.ds(0, n)], c_recv.at[k])
        for s, shift in enumerate(groups[k]):
            gh_s[block_rows(shift), :] = unfold(c_buf[k, :, s])
        gh_out[:, unit_lanes(k)] = jnp.transpose(gh_s[unit_lanes(k), :])[:COLS, :]

    GB = 256

    def rows_grad(b):
        cols = pl.ds(pl.multiple_of(b * GB, GB), GB)
        dquant = jnp.dot(ht_s[:COLS, :], dl_s[:, cols], preferred_element_type=f32)
        usable = (fl1[:, cols] == 0).astype(f32)
        ratios = w_v[:, cols] * (1.0 / sc1[:, cols])
        rounded = jnp.floor(ratios + 0.5)
        levels = jnp.clip(rounded, -8.0, 7.0)
        inside = (rounded == levels).astype(f32)
        gw_out[:, cols] = inside * dquant + (DECAY * usable) * w_v[:, cols]
        terms = jnp.sum(dquant * (levels - inside * ratios), axis=0, keepdims=True)
        for i in range(GB // 128):
            f_buf[w, pl.ds(b * (GB // 128) + i, 1), :] = terms[:, i * 128 : (i + 1) * 128]

    @pl.loop(0, 7)
    def _(i):
        form_dlogits(i - 3)

    stage_a(0)
    stage_a(1)
    stage_a(2)
    ag_last()
    form_dlogits(4)
    stage_a(3)

    @pl.loop(0, 2)
    def _(b):
        rows_grad(b)

    stage_b(0)
    stage_b(1)
    stage_b(2)
    stage_b(3)

    @pl.loop(2, 4)
    def _(b):
        rows_grad(b)

    for j in range(1, NZ):
        pltpu.make_async_remote_copy(
            src_ref=f_buf.at[w], dst_ref=f_buf.at[w], send_sem=f_send, recv_sem=f_recv,
            device_id=z_peer(j), device_id_type=MESH,
        ).start()
    stage_c(0)
    stage_c(1)
    stage_c(2)
    stage_c(3)
    wait_bytes(f_buf.at[pl.ds(0, NZ - 1)], f_recv)
    tail = f_buf[0]
    for i in range(1, NZ):
        tail += f_buf[i]
    gs_out[...] = tail[:8, :] * (1.0 / math.sqrt(D * 7.0))
    loss_out[...] = jnp.sum(tail[8:9, :], axis=1, keepdims=True)
    stage_d(0)
    stage_d(1)
    stage_d(2)
    stage_d(3)

    for k in range(len(groups)):
        n = len(groups[k])
        wait_bytes(a_out.at[k, pl.ds(0, NG - 1), pl.ds(0, n)], a_send.at[k])
        wait_bytes(b_buf.at[k, pl.ds(0, NY - 1), pl.ds(0, n)], b_send.at[k])
        wait_bytes(c_buf.at[k, pl.ds(0, NG - 1), pl.ds(0, n)], c_send.at[k])
    wait_bytes(st_a.at[pl.ds(0, NG - 1)], sa_send)
    wait_bytes(st_b.at[pl.ds(0, NY - 1)], sb_send)
    wait_bytes(st_z.at[pl.ds(0, NZ - 1)], sz_send)
    wait_bytes(f_buf.at[pl.ds(0, NZ - 1)], f_send)
    for way in (0, 1):
        for step in range(4):
            for sub in range(NS):
                if step > 0 or sub in firsts[way]:
                    rs_copy(way, step, sub).wait_send()
                if step < 3 or sub in firsts[way]:
                    ag_copy(way, step, sub).wait_send()


def per_device(hidden, weight, scale, flags, targets):
    f32, bf16, i16 = jnp.float32, jnp.bfloat16, jnp.int16
    vmem = pl.BlockSpec(memory_space=pltpu.VMEM)
    anywhere = pl.BlockSpec(memory_space=pl.ANY)
    dma = pltpu.SemaphoreType.DMA
    grad_weight, grad_scale, grad_hidden, loss = pl.pallas_call(
        kernel,
        out_shape=(
            pltpu.VMEM((COLS, ROWS), f32),
            jax.ShapeDtypeStruct((8, 128), f32),
            pltpu.VMEM((COLS, 512), f32),
            jax.ShapeDtypeStruct((1, 1), f32),
        ),
        in_specs=[anywhere] * 5,
        out_specs=(vmem, vmem, vmem, vmem),
        scratch_shapes=[
            pltpu.VMEM((COLS, ROWS), f32),
            pltpu.VMEM((1, ROWS), f32),
            pltpu.VMEM((1, ROWS), jnp.int32),
            pltpu.VMEM((4, 128), jnp.int32),
            pltpu.VMEM((PAD, 512), bf16),
            pltpu.VMEM((PAD, ROWS), bf16),
            pltpu.VMEM((512, PAD), bf16),
            pltpu.VMEM((512, ROWS), f32),
            pltpu.VMEM((512, ROWS), bf16),
            pltpu.VMEM((128, 128), f32),
            pltpu.VMEM((128, 128), f32),
            pltpu.VMEM((TB, 128), f32),
            pltpu.VMEM((TB, ROWS), f32),
            pltpu.VMEM((2, 4, NS, HB, ROWS + 128), i16),
            pltpu.VMEM((2, 4, NS, HB, ROWS + 128), i16),
            pltpu.VMEM((NZ, NS, HB, ROWS), i16),
            pltpu.VMEM((NG, 8, 128), f32),
            pltpu.VMEM((NY, 8, 128), f32),
            pltpu.VMEM((NZ, 8, 128), f32),
            pltpu.VMEM((512, PAD), f32),
            pltpu.VMEM((4, NG, 3, 16, FOLD), i16),
            pltpu.VMEM((4, NG, 3, 16, FOLD), i16),
            pltpu.VMEM((4, NY, 3, 16, FOLD), i16),
            pltpu.VMEM((4, NG, 3, 16, FOLD), i16),
            pltpu.VMEM((NZ, 16, 128), f32),
            dma((4,)),
            dma(()),
            dma((3,)),
            dma((2, 4, NS)),
            dma((2, 4, NS)),
            dma((2, 4, NS)),
            dma((2, 4, NS)),
            dma(()),
            dma(()),
            dma(()),
            dma(()),
            dma(()),
            dma(()),
            dma((4,)),
            dma((4,)),
            dma((4,)),
            dma((4,)),
            dma((4,)),
            dma((4,)),
            dma(()),
            dma(()),
        ],
        compiler_params=pltpu.CompilerParams(
            collective_id=0, has_side_effects=True, vmem_limit_bytes=58 * 1024 * 1024
        ),
    )(
        hidden.T,
        weight.T,
        scale.reshape(1, ROWS),
        flags.reshape(1, ROWS),
        targets.reshape(4, 128),
    )
    return (grad_weight.T, grad_scale.reshape(ROWS), grad_hidden.T, loss.reshape(()))


def solution(mesh):
    placed = (P(None, "width"), P("vocab", "width"), P("vocab"), P("vocab"), P())
    return jax.shard_map(
        per_device,
        mesh=mesh,
        in_specs=placed,
        out_specs=(P("vocab", "width"), P("vocab"), P(None, "width"), P()),
        check_vma=False,
    )
```

```python
import functools
import math

import jax
import jax.numpy as jnp
from jax import lax
from jax.experimental import pallas as pl
from jax.experimental.pallas import tpu as pltpu
from jax.sharding import PartitionSpec as P

D = 5376
NEG_FILL = -1e30
DECAY = 0.1
MESH = pl.DeviceIdType.MESH

NZ = 8
NG = 8
NY = 4
TB = 64
NS = 4
HB = TB // NS
ROWS = 1024
COLS = 672
PAD = 768
FOLD = 384

CODE_TOP = 32000.0
UNIT = math.log(2.0) / 256.0
ROOT_TOP = 65535.0
ROOT_MID = 32768.0


def code_step(x, top_code, axis):
    top = jnp.max(jnp.abs(x), axis=axis, keepdims=True)
    e = jnp.ceil(jnp.log(jnp.maximum(top, 1e-30) * (1.0 / top_code)) * (1.0 / UNIT))
    return e, jnp.exp(e * (-UNIT))


def to_codes(x, inv):
    return jnp.floor(x * inv + 0.5)


def kernel(
    hid_hbm, w_hbm, sc_hbm, fl_hbm, tg_hbm,
    gw_out, gs_out, gh_out, loss_out,
    w_v, sc1, fl1, tg4, ht_s, q_s, h_s, part, dl_s, tr_s, zt_s, own_s, root_s,
    rs_out, rs_in, ag_s, st_a, st_b, st_z, gh_s, a_out, a_in, b_buf, c_buf, f_buf,
    w_sem, h_sem, small_sem,
    rs_send, rs_recv, ag_send, ag_recv,
    sa_send, sa_recv, sb_send, sb_recv, sz_send, sz_recv,
    a_send, a_recv, b_send, b_recv, c_send, c_recv, f_send, f_recv,
):
    f32, bf16, i32, i16 = jnp.float32, jnp.bfloat16, jnp.int32, jnp.int16
    v = lax.axis_index("vocab")
    w = lax.axis_index("width")
    core = lax.rem(v, 2)
    x = lax.rem(lax.div(v, 2), 4)
    y = lax.div(v, 8)
    right = (v, lax.rem(w + 1, NZ))
    left = (v, lax.rem(w + NZ - 1, NZ))

    def g_index(mode):
        return (x if mode == "x" else y) * 2 + core

    def g_peer(mode, j):
        other = lax.rem(g_index(mode) + j, NG)
        far, far_core = lax.div(other, 2), lax.rem(other, 2)
        if mode == "x":
            return other, ((y * 4 + far) * 2 + far_core, w)
        return other, ((far * 4 + x) * 2 + far_core, w)

    def y_index(mode):
        return y if mode == "x" else x

    def y_peer(mode, j):
        other = lax.rem(y_index(mode) + j, NY)
        if mode == "x":
            return other, ((other * 4 + x) * 2 + core, w)
        return other, ((y * 4 + other) * 2 + core, w)

    def z_peer(j):
        return (v, lax.rem(w + j, NZ))

    def block_rows(shift, half=None):
        block = lax.rem(w + (shift + 2 * NZ), NZ)
        if half is None:
            return pl.ds(pl.multiple_of(block * TB, TB), TB)
        return pl.ds(pl.multiple_of(block * TB + half * HB, HB), HB)

    small_copies = [
        pltpu.make_async_copy(src, dst, small_sem.at[i])
        for i, (src, dst) in enumerate([(tg_hbm, tg4), (sc_hbm, sc1), (fl_hbm, fl1)])
    ]
    for copy in small_copies:
        copy.start()
    WB = 256

    def w_copy(i):
        cols = pl.ds(pl.multiple_of(i * WB, WB), WB)
        return pltpu.make_async_copy(w_hbm.at[:, cols], w_v.at[:, cols], w_sem.at[i])

    @pl.loop(0, ROWS // WB)
    def _(i):
        w_copy(i).start()

    h_copy = pltpu.make_async_copy(hid_hbm, ht_s.at[pl.ds(0, COLS)], h_sem)
    h_copy.start()

    barrier = pltpu.get_barrier_semaphore()
    for j in range(1, NZ):
        pl.semaphore_signal(barrier, inc=1, device_id=z_peer(j), device_id_type=MESH)
    for j in range(1, NG):
        pl.semaphore_signal(
            barrier, inc=1, device_id=g_peer("x", j)[1], device_id_type=MESH
        )
    for j in range(2, NG):
        far = lax.rem(y + lax.div(j, 2), 4)
        pl.semaphore_signal(
            barrier,
            inc=1,
            device_id=((far * 4 + x) * 2 + j % 2, w),
            device_id_type=MESH,
        )

    for copy in small_copies:
        copy.wait()
    tr_s[...] = jnp.transpose(
        jnp.concatenate([tg4[...].astype(f32), jnp.zeros((124, 128), f32)], axis=0)
    )
    ht_s[COLS:, :] = jnp.zeros((PAD - COLS, 512), bf16)
    q_s[COLS:, :] = jnp.zeros((PAD - COLS, ROWS), bf16)
    h_copy.wait()

    @pl.loop(0, ROWS // WB)
    def _(i):
        w_copy(i).wait()
        tokens = pl.ds(pl.multiple_of(i * 128, 128), 128)
        h_s[tokens, :] = jnp.transpose(ht_s[:, tokens])
        cols = pl.ds(pl.multiple_of(i * WB, WB), WB)
        scale = sc1[:, cols]
        rounded = jnp.floor(w_v[:, cols] * (1.0 / scale) + 0.5)
        levels = jnp.clip(rounded, -8.0, 7.0)
        q_s[:COLS, cols] = (scale * levels).astype(bf16)

    def logits_of(shifts):
        rows = [h_s[block_rows(shift), :] for shift in shifts]
        values = jnp.dot(
            jnp.concatenate(rows, axis=0) if len(shifts) > 1 else rows[0],
            q_s[...],
            preferred_element_type=f32,
        )
        for i, shift in enumerate(shifts):
            part[block_rows(shift), :] = values[i * TB : (i + 1) * TB, :]

    logits_of((4,))
    pl.semaphore_wait(barrier, (NZ - 1) + (NG - 1) + (NG - 2))

    lane_half = lax.broadcasted_iota(i32, (HB, 128), 1)

    def rs_copy(way, step, half):
        return pltpu.make_async_remote_copy(
            src_ref=rs_out.at[way, step, half],
            dst_ref=rs_in.at[way, step, half],
            send_sem=rs_send.at[way, step, half],
            recv_sem=rs_recv.at[way, step, half],
            device_id=right if way == 0 else left,
            device_id_type=MESH,
        )

    def encode(value, ref):
        e, inv = code_step(value, 4.0 * CODE_TOP, 1)
        codes = to_codes(value, inv).astype(i32)
        ref[:, :ROWS] = (codes >> 2).astype(i16)
        low = codes & 3
        pairs = low[:, :128]
        for i in range(1, ROWS // 128):
            pairs = pairs | (low[:, i * 128 : (i + 1) * 128] << (2 * i))
        ref[:, ROWS:] = jnp.where(lane_half == 0, e.astype(i32), pairs).astype(i16)

    def decode(ref):
        high = ref[:, :ROWS].astype(i32) << 2
        pairs = ref[:, ROWS:].astype(i32)
        unit = jnp.exp(pairs[:, :1].astype(f32) * UNIT)
        blocks = []
        for i in range(ROWS // 128):
            low = jnp.where(lane_half == 0, 1.5, ((pairs >> (2 * i)) & 3).astype(f32))
            blocks.append(high[:, i * 128 : (i + 1) * 128].astype(f32) + low)
        return jnp.concatenate(blocks, axis=1) * unit

    def rs_get(way, step, sub):
        return decode(rs_in.at[way, step, sub])

    def mine(shift, half):
        return part[block_rows(shift, half), :]

    firsts = ([s for s in range(NS) if s < NS // 2], [s for s in range(NS) if s >= NS // 2])

    def rs_pair(n, add):
        step = lax.div(n, NS)
        subs = (lax.rem(n + NS // 2, NS), lax.rem(n, NS))
        if add:
            for way in (0, 1):
                rs_copy(way, step - 1, subs[way]).wait_recv()
        values = [mine(4 - step, subs[0]), mine(step - 4, subs[1])]
        if add:
            values = [values[way] + rs_get(way, step - 1, subs[way]) for way in (0, 1)]
        for way in (0, 1):
            encode(values[way], rs_out.at[way, step, subs[way]])
        for way in (0, 1):
            rs_copy(way, step, subs[way]).start()

    @pl.loop(NS // 2, NS)
    def _(n):
        rs_pair(n, False)

    logits_of((3, -3))

    @pl.loop(NS, NS + NS // 2)
    def _(n):
        rs_pair(n, False)

    logits_of((2, -2))

    @pl.loop(NS + NS // 2, 2 * NS)
    def _(n):
        rs_pair(n, True)

    logits_of((1, -1, 0))

    @pl.loop(2 * NS, 4 * NS)
    def _(n):
        rs_pair(n, True)

    def ag_ref(way, step, sub):
        block = lax.rem(w + (step if way == 1 else NZ - step), NZ)
        return ag_s.at[block, sub]

    def ag_copy(way, step, sub):
        ref = ag_ref(way, step, sub)
        return pltpu.make_async_remote_copy(
            src_ref=ref,
            dst_ref=ref,
            send_sem=ag_send.at[way, step, sub],
            recv_sem=ag_recv.at[way, step, sub],
            device_id=right if way == 0 else left,
            device_id_type=MESH,
        )

    def ag_wait(way, step, sub):
        ref = ag_ref(way, step + 1, sub)
        pltpu.make_async_copy(ref, ref, ag_recv.at[way, step, sub]).wait()

    def ag_step(step):
        for sub in range(NS):
            for way in (0, 1):
                ag_wait(way, step, sub)
                if sub in firsts[way]:
                    ag_copy(way, step + 1, sub).start()
                else:

                    @pl.when(step < 2)
                    def _():
                        ag_copy(way, step + 1, sub).start()

    def ag_last():
        for way in (0, 1):
            for sub in firsts[way]:
                ag_wait(way, 3, sub)

    usable_row = fl1[...] == 0

    def pick_lane(ref, index, rows):
        at = lax.broadcasted_iota(i32, (rows.size, 128), 1)
        return jnp.sum(jnp.where(at == index, ref[rows, :], 0.0), axis=1, keepdims=True)

    def hits(block, first, count):
        rows = pl.ds(pl.multiple_of(lax.rem(block, 2) * TB + first, count), count)
        column = pick_lane(tr_s, lax.div(block, 2), rows).astype(i32) - v * ROWS
        return lax.broadcasted_iota(i32, (count, ROWS), 1) == column

    @pl.loop(0, NS)
    def _(sub):
        for way in (0, 1):
            rs_copy(way, 3, sub).wait_recv()
        own = mine(0, sub) + rs_get(0, 3, sub) + rs_get(1, 3, sub)
        masked = jnp.where(usable_row, own, NEG_FILL)
        top = jnp.max(masked, axis=1, keepdims=True)
        root = jnp.where(usable_row, jnp.exp((masked - top) * 0.5), 0.0)
        codes = jnp.floor(root * ROOT_TOP + (0.5 - ROOT_MID))
        ag_s[w, sub] = codes.astype(i32).astype(i16)
        for way in (0, 1):
            ag_copy(way, 0, sub).start()
        rows = pl.ds(pl.multiple_of(sub * HB, HB), HB)
        part[block_rows(0, sub), :] = own
        root_s[rows, :] = root
        own_s[rows, :] = jnp.broadcast_to(top, (HB, 128))

    lane = lax.broadcasted_iota(i32, (TB, 128), 1)
    total = jnp.sum(root_s[...] * root_s[...], axis=1, keepdims=True)
    picked = jnp.sum(
        jnp.where(hits(w, 0, TB), part[block_rows(0), :], 0.0), axis=1, keepdims=True
    )
    stats = jnp.where(
        lane == 0,
        own_s[...],
        jnp.where(lane == 1, total, jnp.where(lane == 2, picked, 0.0)),
    )

    stats = jnp.transpose(jnp.concatenate([stats, jnp.zeros((TB, 128), f32)], axis=0))
    g = g_index("x")
    st_a[g] = stats[:8, :]
    for j in range(1, NG):
        pltpu.make_async_remote_copy(
            src_ref=st_a.at[g], dst_ref=st_a.at[g], send_sem=sa_send, recv_sem=sa_recv,
            device_id=g_peer("x", j)[1], device_id_type=MESH,
        ).start()

    def wait_bytes(ref, sem):
        pltpu.make_async_copy(ref, ref, sem).wait()

    def merge(buf, n):
        best = buf[0, 0:1, :]
        for i in range(1, n):
            best = jnp.maximum(best, buf[i, 0:1, :])
        weight = jnp.zeros((1, 128), f32)
        pick = jnp.zeros((1, 128), f32)
        for i in range(n):
            weight += buf[i, 1:2, :] * jnp.exp(buf[i, 0:1, :] - best)
            pick += buf[i, 2:3, :]
        return best, weight, pick

    def form_dlogits(shift):
        block = lax.rem(w + (shift + NZ), NZ)
        factor = pick_lane(zt_s, block, pl.ds(0, TB))
        dl_s[block_rows(shift), :] = (
            part[block_rows(shift), :] * factor - hits(block, 0, TB).astype(f32)
        ).astype(bf16)

    def form_squares(shift):
        block = lax.rem(w + (shift + NZ), NZ)
        codes = jnp.concatenate([ag_s[block, s] for s in range(NS)], axis=0)
        root = codes.astype(i32).astype(f32) + ROOT_MID
        part[block_rows(shift), :] = root * root

    groups = [(0,), (-1, 1), (-2, 2), (-3, 3), (4,)]
    modes = ["x", "x", "y", "y", "x"]
    nt = (((1,), (1,)), ((), ()))

    def fold(x):
        n = x.shape[0] // 8
        e, inv = code_step(x, CODE_TOP, 1)
        wide = lax.broadcasted_iota(i32, (8 * n, PAD), 1)
        codes = jnp.where(wide < COLS, to_codes(x, inv), e).astype(i32)
        return jnp.concatenate(
            [codes[:, :FOLD].reshape(n, 8, FOLD), codes[:, FOLD:].reshape(n, 8, FOLD)], axis=1
        ).astype(i16)

    def unfold(piece):
        n = piece.shape[0]
        codes = piece.astype(i32).astype(f32)
        low = codes[:, :8, :].reshape(8 * n, FOLD)
        high = codes[:, 8:, :].reshape(8 * n, FOLD)
        unit = jnp.exp(high[:, FOLD - 1 :] * UNIT)
        wide = jnp.concatenate([low, high], axis=1)
        lane_pad = lax.broadcasted_iota(i32, (8 * n, PAD), 1)
        return jnp.where(lane_pad < COLS, wide * unit, 0.0)

    def stage_a(k):
        n = len(groups[k])
        for shift in groups[k]:
            form_dlogits(shift)
        terms = [dl_s[block_rows(shift), :] for shift in groups[k]]
        term = lax.dot_general(
            jnp.concatenate(terms, axis=0) if n > 1 else terms[0],
            q_s[...],
            nt,
            preferred_element_type=f32,
        )
        g = g_index(modes[k])
        for s in range(n):
            a_out[k, :, s] = fold(term[s * TB : (s + 1) * TB])
        a_in[k, g] = a_out[k, g]
        for j in range(1, NG):
            other, device = g_peer(modes[k], j)
            pltpu.make_async_remote_copy(
                src_ref=a_out.at[k, other, pl.ds(0, n)], dst_ref=a_in.at[k, g, pl.ds(0, n)],
                send_sem=a_send.at[k], recv_sem=a_recv.at[k],
                device_id=device, device_id_type=MESH,
            ).start()

    def stage_b(k):
        n = len(groups[k])
        wait_bytes(a_in.at[k, pl.ds(0, NG - 1), pl.ds(0, n)], a_recv.at[k])
        total = unfold(a_in[k, 0, :n])
        for i in range(1, NG):
            total += unfold(a_in[k, i, :n])
        at = y_index(modes[k])
        b_buf[k, at, :n] = fold(total)
        for j in range(1, NY):
            mine_ref = b_buf.at[k, at, pl.ds(0, n)]
            pltpu.make_async_remote_copy(
                src_ref=mine_ref, dst_ref=mine_ref,
                send_sem=b_send.at[k], recv_sem=b_recv.at[k],
                device_id=y_peer(modes[k], j)[1], device_id_type=MESH,
            ).start()

    def stage_c(k):
        n = len(groups[k])
        wait_bytes(b_buf.at[k, pl.ds(0, NY - 1), pl.ds(0, n)], b_recv.at[k])
        total = unfold(b_buf[k, 0, :n])
        for i in range(1, NY):
            total += unfold(b_buf[k, i, :n])
        g = g_index(modes[k])
        c_buf[k, g, :n] = fold(total)
        for j in range(1, NG):
            mine_ref = c_buf.at[k, g, pl.ds(0, n)]
            pltpu.make_async_remote_copy(
                src_ref=mine_ref, dst_ref=mine_ref,
                send_sem=c_send.at[k], recv_sem=c_recv.at[k],
                device_id=g_peer(modes[k], j)[1], device_id_type=MESH,
            ).start()

    odd = lax.rem(w, 2)
    unit_blocks = [w, w + 2 * odd - 1, w + 2 - 4 * odd, w + 4]

    def unit_lanes(k):
        unit = lax.div(lax.rem(unit_blocks[k] + NZ, NZ), 2)
        return pl.ds(pl.multiple_of(unit * 128, 128), 128)

    def stage_d(k):
        n = len(groups[k])
        wait_bytes(c_buf.at[k, pl.ds(0, NG - 1), pl.ds(0, n)], c_recv.at[k])
        for s, shift in enumerate(groups[k]):
            gh_s[block_rows(shift), :] = unfold(c_buf[k, :, s])
        if k > 0:
            pair = unit_lanes(k - 1)
            gh_out[:, pair] = jnp.transpose(gh_s[pair, :])[:COLS, :]

    GB = 256

    def rows_grad(b):
        cols = pl.ds(pl.multiple_of(b * GB, GB), GB)
        dquant = jnp.dot(ht_s[:COLS, :], dl_s[:, cols], preferred_element_type=f32)
        usable = (fl1[:, cols] == 0).astype(f32)
        ratios = w_v[:, cols] * (1.0 / sc1[:, cols])
        rounded = jnp.floor(ratios + 0.5)
        levels = jnp.clip(rounded, -8.0, 7.0)
        inside = (rounded == levels).astype(f32)
        gw_out[:, cols] = inside * dquant + (DECAY * usable) * w_v[:, cols]
        terms = jnp.sum(dquant * (levels - inside * ratios), axis=0, keepdims=True)
        for i in range(GB // 128):
            f_buf[w, pl.ds(b * (GB // 128) + i, 1), :] = terms[:, i * 128 : (i + 1) * 128]

    @pl.loop(0, 3)
    def _(step):
        ag_step(step)

        @pl.loop(0, 2)
        def _(side):
            form_squares((step + 1) * (2 * side - 1))

        @pl.when(step == 0)
        def _():
            wait_bytes(st_a.at[pl.ds(0, NG - 1)], sa_recv)
            best, weight, pick = merge(st_a, NG)
            st_b[y] = jnp.concatenate([best, weight, pick, jnp.zeros((5, 128), f32)], axis=0)
            for j in range(1, NY):
                pltpu.make_async_remote_copy(
                    src_ref=st_b.at[y], dst_ref=st_b.at[y], send_sem=sb_send, recv_sem=sb_recv,
                    device_id=y_peer("x", j)[1], device_id_type=MESH,
                ).start()

        @pl.when(step == 1)
        def _():
            wait_bytes(st_b.at[pl.ds(0, NY - 1)], sb_recv)
            best, weight, pick = merge(st_b, NY)
            lane_row = lax.broadcasted_iota(i32, (1, 128), 1)
            loss_row = jnp.where(lane_row < TB, best + jnp.log(weight) - pick, 0.0)
            f_buf[w, pl.ds(8, 8), :] = jnp.broadcast_to(loss_row, (8, 128))
            factor = jnp.exp(st_a[g, 0:1, :] - best) / weight
            factor = factor * (1.0 / (ROOT_TOP * ROOT_TOP))
            st_z[w] = jnp.broadcast_to(factor, (8, 128))
            for j in range(1, NZ):
                pltpu.make_async_remote_copy(
                    src_ref=st_z.at[w], dst_ref=st_z.at[w], send_sem=sz_send, recv_sem=sz_recv,
                    device_id=z_peer(j), device_id_type=MESH,
                ).start()
            zt_s[...] = jnp.transpose(jnp.broadcast_to(factor, (128, 128)))
            form_squares(0)
            stage_a(0)

    wait_bytes(st_z.at[pl.ds(0, NZ - 1)], sz_recv)
    rows_of = [st_z[i, 0:1, :] for i in range(NZ)]
    zt_s[...] = jnp.transpose(
        jnp.concatenate(rows_of + [jnp.zeros((120, 128), f32)], axis=0)
    )

    stage_a(1)
    stage_a(2)
    stage_a(3)
    ag_last()
    form_squares(4)
    stage_a(4)

    @pl.loop(0, 2)
    def _(b):
        rows_grad(b)

    stage_b(0)
    stage_b(1)
    stage_b(2)
    stage_b(3)
    stage_b(4)

    @pl.loop(2, 4)
    def _(b):
        rows_grad(b)

    for j in range(1, NZ):
        pltpu.make_async_remote_copy(
            src_ref=f_buf.at[w], dst_ref=f_buf.at[w], send_sem=f_send, recv_sem=f_recv,
            device_id=z_peer(j), device_id_type=MESH,
        ).start()
    stage_c(0)
    stage_c(1)
    stage_c(2)
    stage_c(3)
    stage_c(4)
    wait_bytes(f_buf.at[pl.ds(0, NZ - 1)], f_recv)
    tail = f_buf[0]
    for i in range(1, NZ):
        tail += f_buf[i]
    gs_out[...] = tail[:8, :] * (1.0 / math.sqrt(D * 7.0))
    loss_out[...] = jnp.sum(tail[8:9, :], axis=1, keepdims=True)
    stage_d(0)
    stage_d(1)
    stage_d(2)
    stage_d(3)
    stage_d(4)

    for k in range(len(groups)):
        n = len(groups[k])
        wait_bytes(a_out.at[k, pl.ds(0, NG - 1), pl.ds(0, n)], a_send.at[k])
        wait_bytes(b_buf.at[k, pl.ds(0, NY - 1), pl.ds(0, n)], b_send.at[k])
        wait_bytes(c_buf.at[k, pl.ds(0, NG - 1), pl.ds(0, n)], c_send.at[k])
    wait_bytes(st_a.at[pl.ds(0, NG - 1)], sa_send)
    wait_bytes(st_b.at[pl.ds(0, NY - 1)], sb_send)
    wait_bytes(st_z.at[pl.ds(0, NZ - 1)], sz_send)
    wait_bytes(f_buf.at[pl.ds(0, NZ - 1)], f_send)
    for way in (0, 1):
        for step in range(4):
            for sub in range(NS):
                if step > 0 or sub in firsts[way]:
                    rs_copy(way, step, sub).wait_send()
                if step < 3 or sub in firsts[way]:
                    ag_copy(way, step, sub).wait_send()


def per_device(hidden, weight, scale, flags, targets):
    f32, bf16, i16 = jnp.float32, jnp.bfloat16, jnp.int16
    vmem = pl.BlockSpec(memory_space=pltpu.VMEM)
    anywhere = pl.BlockSpec(memory_space=pl.ANY)
    dma = pltpu.SemaphoreType.DMA
    grad_weight, grad_scale, grad_hidden, loss = pl.pallas_call(
        kernel,
        out_shape=(
            pltpu.VMEM((COLS, ROWS), f32),
            jax.ShapeDtypeStruct((8, 128), f32),
            pltpu.VMEM((COLS, 512), f32),
            jax.ShapeDtypeStruct((1, 1), f32),
        ),
        in_specs=[anywhere] * 5,
        out_specs=(vmem, vmem, vmem, vmem),
        scratch_shapes=[
            pltpu.VMEM((COLS, ROWS), f32),
            pltpu.VMEM((1, ROWS), f32),
            pltpu.VMEM((1, ROWS), jnp.int32),
            pltpu.VMEM((4, 128), jnp.int32),
            pltpu.VMEM((PAD, 512), bf16),
            pltpu.VMEM((PAD, ROWS), bf16),
            pltpu.VMEM((512, PAD), bf16),
            pltpu.VMEM((512, ROWS), f32),
            pltpu.VMEM((512, ROWS), bf16),
            pltpu.VMEM((128, 128), f32),
            pltpu.VMEM((128, 128), f32),
            pltpu.VMEM((TB, 128), f32),
            pltpu.VMEM((TB, ROWS), f32),
            pltpu.VMEM((2, 4, NS, HB, ROWS + 128), i16),
            pltpu.VMEM((2, 4, NS, HB, ROWS + 128), i16),
            pltpu.VMEM((NZ, NS, HB, ROWS), i16),
            pltpu.VMEM((NG, 8, 128), f32),
            pltpu.VMEM((NY, 8, 128), f32),
            pltpu.VMEM((NZ, 8, 128), f32),
            pltpu.VMEM((512, PAD), f32),
            pltpu.VMEM((5, NG, 2, 16, FOLD), i16),
            pltpu.VMEM((5, NG, 2, 16, FOLD), i16),
            pltpu.VMEM((5, NY, 2, 16, FOLD), i16),
            pltpu.VMEM((5, NG, 2, 16, FOLD), i16),
            pltpu.VMEM((NZ, 16, 128), f32),
            dma((4,)),
            dma(()),
            dma((3,)),
            dma((2, 4, NS)),
            dma((2, 4, NS)),
            dma((2, 4, NS)),
            dma((2, 4, NS)),
            dma(()),
            dma(()),
            dma(()),
            dma(()),
            dma(()),
            dma(()),
            dma((5,)),
            dma((5,)),
            dma((5,)),
            dma((5,)),
            dma((5,)),
            dma((5,)),
            dma(()),
            dma(()),
        ],
        compiler_params=pltpu.CompilerParams(
            collective_id=0, has_side_effects=True, vmem_limit_bytes=58 * 1024 * 1024
        ),
    )(
        hidden.T,
        weight.T,
        scale.reshape(1, ROWS),
        flags.reshape(1, ROWS),
        targets.reshape(4, 128),
    )
    return (grad_weight.T, grad_scale.reshape(ROWS), grad_hidden.T, loss.reshape(()))


def solution(mesh):
    placed = (P(None, "width"), P("vocab", "width"), P("vocab"), P("vocab"), P())
    return jax.shard_map(
        per_device,
        mesh=mesh,
        in_specs=placed,
        out_specs=(P("vocab", "width"), P("vocab"), P(None, "width"), P()),
        check_vma=False,
    )
```

```python
import functools
import math

import jax
import jax.numpy as jnp
from jax import lax
from jax.experimental import pallas as pl
from jax.experimental.pallas import tpu as pltpu
from jax.sharding import PartitionSpec as P

D = 5376
NEG_FILL = -1e30
DECAY = 0.1
MESH = pl.DeviceIdType.MESH

NZ = 8
NG = 8
NY = 4
TB = 64
NS = 4
HB = TB // NS
ROWS = 1024
COLS = 672
PAD = 768
FOLD = 384

CODE_TOP = 32000.0
UNIT = math.log(2.0) / 256.0
ROOT_TOP = 65535.0
ROOT_MID = 32768.0


def code_step(x, top_code, axis):
    top = jnp.max(jnp.abs(x), axis=axis, keepdims=True)
    e = jnp.ceil(jnp.log(jnp.maximum(top, 1e-30) * (1.0 / top_code)) * (1.0 / UNIT))
    return e, jnp.exp(e * (-UNIT))


def to_codes(x, inv):
    return jnp.floor(x * inv + 0.5)


def kernel(
    hid_hbm, w_hbm, sc_hbm, fl_hbm, tg_hbm,
    gw_out, gs_hbm, gh_out, loss_hbm,
    gs_out, loss_out, w_v, sc1, fl1, tg4, ht_s, q_s, h_s, part, dl_s, tr_s, zt_s, own_s, root_s,
    rs_out, rs_in, ag_s, st_a, st_b, st_z, gh_s, a_out, a_in, b_buf, c_buf, f_buf,
    w_sem, h_sem, small_sem, end_sem,
    rs_send, rs_recv, ag_send, ag_recv,
    sa_send, sa_recv, sb_send, sb_recv, sz_send, sz_recv,
    a_send, a_recv, b_send, b_recv, c_send, c_recv, f_send, f_recv,
):
    f32, bf16, i32, i16 = jnp.float32, jnp.bfloat16, jnp.int32, jnp.int16
    v = lax.axis_index("vocab")
    w = lax.axis_index("width")
    core = lax.rem(v, 2)
    x = lax.rem(lax.div(v, 2), 4)
    y = lax.div(v, 8)
    right = (v, lax.rem(w + 1, NZ))
    left = (v, lax.rem(w + NZ - 1, NZ))

    def g_index(mode):
        return (x if mode == "x" else y) * 2 + core

    def g_peer(mode, j):
        other = lax.rem(g_index(mode) + j, NG)
        far, far_core = lax.div(other, 2), lax.rem(other, 2)
        if mode == "x":
            return other, ((y * 4 + far) * 2 + far_core, w)
        return other, ((far * 4 + x) * 2 + far_core, w)

    def y_index(mode):
        return y if mode == "x" else x

    def y_peer(mode, j):
        other = lax.rem(y_index(mode) + j, NY)
        if mode == "x":
            return other, ((other * 4 + x) * 2 + core, w)
        return other, ((y * 4 + other) * 2 + core, w)

    def z_peer(j):
        return (v, lax.rem(w + j, NZ))

    def block_rows(shift, half=None):
        block = lax.rem(w + (shift + 2 * NZ), NZ)
        if half is None:
            return pl.ds(pl.multiple_of(block * TB, TB), TB)
        return pl.ds(pl.multiple_of(block * TB + half * HB, HB), HB)

    small_copies = [
        pltpu.make_async_copy(src, dst, small_sem.at[i])
        for i, (src, dst) in enumerate([(tg_hbm, tg4), (sc_hbm, sc1), (fl_hbm, fl1)])
    ]
    for copy in small_copies:
        copy.start()
    WB = 256

    def w_copy(i):
        cols = pl.ds(pl.multiple_of(i * WB, WB), WB)
        return pltpu.make_async_copy(w_hbm.at[:, cols], w_v.at[:, cols], w_sem.at[i])

    @pl.loop(0, ROWS // WB)
    def _(i):
        w_copy(i).start()

    h_copy = pltpu.make_async_copy(hid_hbm, ht_s.at[pl.ds(0, COLS)], h_sem)
    h_copy.start()

    barrier = pltpu.get_barrier_semaphore()
    for j in range(1, NZ):
        pl.semaphore_signal(barrier, inc=1, device_id=z_peer(j), device_id_type=MESH)
    for j in range(1, NG):
        pl.semaphore_signal(
            barrier, inc=1, device_id=g_peer("x", j)[1], device_id_type=MESH
        )
    for j in range(2, NG):
        far = lax.rem(y + lax.div(j, 2), 4)
        pl.semaphore_signal(
            barrier,
            inc=1,
            device_id=((far * 4 + x) * 2 + j % 2, w),
            device_id_type=MESH,
        )

    for copy in small_copies:
        copy.wait()
    tr_s[...] = jnp.transpose(
        jnp.concatenate([tg4[...].astype(f32), jnp.zeros((124, 128), f32)], axis=0)
    )
    ht_s[COLS:, :] = jnp.zeros((PAD - COLS, 512), bf16)
    q_s[COLS:, :] = jnp.zeros((PAD - COLS, ROWS), bf16)
    h_copy.wait()

    @pl.loop(0, ROWS // WB)
    def _(i):
        w_copy(i).wait()
        tokens = pl.ds(pl.multiple_of(i * 128, 128), 128)
        h_s[tokens, :] = jnp.transpose(ht_s[:, tokens])
        cols = pl.ds(pl.multiple_of(i * WB, WB), WB)
        scale = sc1[:, cols]
        rounded = jnp.floor(w_v[:, cols] * (1.0 / scale) + 0.5)
        levels = jnp.clip(rounded, -8.0, 7.0)
        q_s[:COLS, cols] = (scale * levels).astype(bf16)

    def logits_of(shifts):
        rows = [h_s[block_rows(shift), :] for shift in shifts]
        values = jnp.dot(
            jnp.concatenate(rows, axis=0) if len(shifts) > 1 else rows[0],
            q_s[...],
            preferred_element_type=f32,
        )
        for i, shift in enumerate(shifts):
            part[block_rows(shift), :] = values[i * TB : (i + 1) * TB, :]

    logits_of((4,))
    pl.semaphore_wait(barrier, (NZ - 1) + (NG - 1) + (NG - 2))

    lane_half = lax.broadcasted_iota(i32, (HB, 128), 1)

    def rs_copy(way, step, half):
        return pltpu.make_async_remote_copy(
            src_ref=rs_out.at[way, step, half],
            dst_ref=rs_in.at[way, step, half],
            send_sem=rs_send.at[way, step, half],
            recv_sem=rs_recv.at[way, step, half],
            device_id=right if way == 0 else left,
            device_id_type=MESH,
        )

    def encode(value, ref):
        e, inv = code_step(value, 4.0 * CODE_TOP, 1)
        codes = to_codes(value, inv).astype(i32)
        ref[:, :ROWS] = (codes >> 2).astype(i16)
        low = codes & 3
        pairs = low[:, :128]
        for i in range(1, ROWS // 128):
            pairs = pairs | (low[:, i * 128 : (i + 1) * 128] << (2 * i))
        ref[:, ROWS:] = jnp.where(lane_half == 0, e.astype(i32), pairs).astype(i16)

    def decode(ref):
        high = ref[:, :ROWS].astype(i32) << 2
        pairs = ref[:, ROWS:].astype(i32)
        unit = jnp.exp(pairs[:, :1].astype(f32) * UNIT)
        blocks = []
        for i in range(ROWS // 128):
            low = jnp.where(lane_half == 0, 1.5, ((pairs >> (2 * i)) & 3).astype(f32))
            blocks.append(high[:, i * 128 : (i + 1) * 128].astype(f32) + low)
        return jnp.concatenate(blocks, axis=1) * unit

    def rs_get(way, step, sub):
        return decode(rs_in.at[way, step, sub])

    def mine(shift, half):
        return part[block_rows(shift, half), :]

    firsts = ([s for s in range(NS) if s < NS // 2], [s for s in range(NS) if s >= NS // 2])

    def rs_pair(n, add):
        step = lax.div(n, NS)
        subs = (lax.rem(n + NS // 2, NS), lax.rem(n, NS))
        if add:
            for way in (0, 1):
                rs_copy(way, step - 1, subs[way]).wait_recv()
        values = [mine(4 - step, subs[0]), mine(step - 4, subs[1])]
        if add:
            values = [values[way] + rs_get(way, step - 1, subs[way]) for way in (0, 1)]
        for way in (0, 1):
            encode(values[way], rs_out.at[way, step, subs[way]])
        for way in (0, 1):
            rs_copy(way, step, subs[way]).start()

    @pl.loop(NS // 2, NS)
    def _(n):
        rs_pair(n, False)

    logits_of((3, -3))

    @pl.loop(NS, NS + NS // 2)
    def _(n):
        rs_pair(n, False)

    logits_of((2, -2))

    @pl.loop(NS + NS // 2, 2 * NS)
    def _(n):
        rs_pair(n, True)

    logits_of((1, -1, 0))

    @pl.loop(2 * NS, 4 * NS)
    def _(n):
        rs_pair(n, True)

    def ag_ref(way, step, sub):
        block = lax.rem(w + (step if way == 1 else NZ - step), NZ)
        return ag_s.at[block, sub]

    def ag_copy(way, step, sub):
        ref = ag_ref(way, step, sub)
        return pltpu.make_async_remote_copy(
            src_ref=ref,
            dst_ref=ref,
            send_sem=ag_send.at[way, step, sub],
            recv_sem=ag_recv.at[way, step, sub],
            device_id=right if way == 0 else left,
            device_id_type=MESH,
        )

    def ag_wait(way, step, sub):
        ref = ag_ref(way, step + 1, sub)
        pltpu.make_async_copy(ref, ref, ag_recv.at[way, step, sub]).wait()

    def ag_step(step):
        for sub in range(NS):
            for way in (0, 1):
                ag_wait(way, step, sub)
                if sub in firsts[way]:
                    ag_copy(way, step + 1, sub).start()
                else:

                    @pl.when(step < 2)
                    def _():
                        ag_copy(way, step + 1, sub).start()

    def ag_last():
        for way in (0, 1):
            for sub in firsts[way]:
                ag_wait(way, 3, sub)

    usable_row = fl1[...] == 0

    def pick_lane(ref, index, rows):
        at = lax.broadcasted_iota(i32, (rows.size, 128), 1)
        return jnp.sum(jnp.where(at == index, ref[rows, :], 0.0), axis=1, keepdims=True)

    def hits(block, first, count):
        rows = pl.ds(pl.multiple_of(lax.rem(block, 2) * TB + first, count), count)
        column = pick_lane(tr_s, lax.div(block, 2), rows).astype(i32) - v * ROWS
        return lax.broadcasted_iota(i32, (count, ROWS), 1) == column

    @pl.loop(0, NS)
    def _(sub):
        for way in (0, 1):
            rs_copy(way, 3, sub).wait_recv()
        own = mine(0, sub) + rs_get(0, 3, sub) + rs_get(1, 3, sub)
        masked = jnp.where(usable_row, own, NEG_FILL)
        top = jnp.max(masked, axis=1, keepdims=True)
        root = jnp.where(usable_row, jnp.exp((masked - top) * 0.5), 0.0)
        codes = jnp.floor(root * ROOT_TOP + (0.5 - ROOT_MID))
        ag_s[w, sub] = codes.astype(i32).astype(i16)
        for way in (0, 1):
            ag_copy(way, 0, sub).start()
        rows = pl.ds(pl.multiple_of(sub * HB, HB), HB)
        part[block_rows(0, sub), :] = own
        root_s[rows, :] = root
        own_s[rows, :] = jnp.broadcast_to(top, (HB, 128))

    lane = lax.broadcasted_iota(i32, (TB, 128), 1)
    total = jnp.sum(root_s[...] * root_s[...], axis=1, keepdims=True)
    picked = jnp.sum(
        jnp.where(hits(w, 0, TB), part[block_rows(0), :], 0.0), axis=1, keepdims=True
    )
    stats = jnp.where(
        lane == 0,
        own_s[...],
        jnp.where(lane == 1, total, jnp.where(lane == 2, picked, 0.0)),
    )

    stats = jnp.transpose(jnp.concatenate([stats, jnp.zeros((TB, 128), f32)], axis=0))
    g = g_index("x")
    st_a[g] = stats[:8, :]
    for j in range(1, NG):
        pltpu.make_async_remote_copy(
            src_ref=st_a.at[g], dst_ref=st_a.at[g], send_sem=sa_send, recv_sem=sa_recv,
            device_id=g_peer("x", j)[1], device_id_type=MESH,
        ).start()

    def wait_bytes(ref, sem):
        pltpu.make_async_copy(ref, ref, sem).wait()

    def merge(buf, n):
        best = buf[0, 0:1, :]
        for i in range(1, n):
            best = jnp.maximum(best, buf[i, 0:1, :])
        weight = jnp.zeros((1, 128), f32)
        pick = jnp.zeros((1, 128), f32)
        for i in range(n):
            weight += buf[i, 1:2, :] * jnp.exp(buf[i, 0:1, :] - best)
            pick += buf[i, 2:3, :]
        return best, weight, pick

    def form_dlogits(shift):
        block = lax.rem(w + (shift + NZ), NZ)
        factor = pick_lane(zt_s, block, pl.ds(0, TB))
        dl_s[block_rows(shift), :] = (
            part[block_rows(shift), :] * factor - hits(block, 0, TB).astype(f32)
        ).astype(bf16)

    def form_squares(shift):
        block = lax.rem(w + (shift + NZ), NZ)
        codes = jnp.concatenate([ag_s[block, s] for s in range(NS)], axis=0)
        root = codes.astype(i32).astype(f32) + ROOT_MID
        part[block_rows(shift), :] = root * root

    groups = [(0,), (-1, 1), (-2, 2), (-3, 3), (4,)]
    modes = ["x", "x", "y", "y", "x"]
    nt = (((1,), (1,)), ((), ()))

    def fold(x):
        n = x.shape[0] // 8
        e, inv = code_step(x, CODE_TOP, 1)
        wide = lax.broadcasted_iota(i32, (8 * n, PAD), 1)
        codes = jnp.where(wide < COLS, to_codes(x, inv), e).astype(i32)
        return jnp.concatenate(
            [codes[:, :FOLD].reshape(n, 8, FOLD), codes[:, FOLD:].reshape(n, 8, FOLD)], axis=1
        ).astype(i16)

    def unfold(piece):
        n = piece.shape[0]
        codes = piece.astype(i32).astype(f32)
        low = codes[:, :8, :].reshape(8 * n, FOLD)
        high = codes[:, 8:, :].reshape(8 * n, FOLD)
        unit = jnp.exp(high[:, FOLD - 1 :] * UNIT)
        wide = jnp.concatenate([low, high], axis=1)
        lane_pad = lax.broadcasted_iota(i32, (8 * n, PAD), 1)
        return jnp.where(lane_pad < COLS, wide * unit, 0.0)

    def stage_a(k):
        n = len(groups[k])
        for shift in groups[k]:
            form_dlogits(shift)
        terms = [dl_s[block_rows(shift), :] for shift in groups[k]]
        term = lax.dot_general(
            jnp.concatenate(terms, axis=0) if n > 1 else terms[0],
            q_s[...],
            nt,
            preferred_element_type=f32,
        )
        g = g_index(modes[k])
        for s in range(n):
            a_out[k, :, s] = fold(term[s * TB : (s + 1) * TB])
        a_in[k, g] = a_out[k, g]
        for j in range(1, NG):
            other, device = g_peer(modes[k], j)
            pltpu.make_async_remote_copy(
                src_ref=a_out.at[k, other, pl.ds(0, n)], dst_ref=a_in.at[k, g, pl.ds(0, n)],
                send_sem=a_send.at[k], recv_sem=a_recv.at[k],
                device_id=device, device_id_type=MESH,
            ).start()

    def stage_b(k):
        n = len(groups[k])
        wait_bytes(a_in.at[k, pl.ds(0, NG - 1), pl.ds(0, n)], a_recv.at[k])
        total = unfold(a_in[k, 0, :n])
        for i in range(1, NG):
            total += unfold(a_in[k, i, :n])
        at = y_index(modes[k])
        b_buf[k, at, :n] = fold(total)
        for j in range(1, NY):
            mine_ref = b_buf.at[k, at, pl.ds(0, n)]
            pltpu.make_async_remote_copy(
                src_ref=mine_ref, dst_ref=mine_ref,
                send_sem=b_send.at[k], recv_sem=b_recv.at[k],
                device_id=y_peer(modes[k], j)[1], device_id_type=MESH,
            ).start()

    def stage_c(k):
        n = len(groups[k])
        wait_bytes(b_buf.at[k, pl.ds(0, NY - 1), pl.ds(0, n)], b_recv.at[k])
        total = unfold(b_buf[k, 0, :n])
        for i in range(1, NY):
            total += unfold(b_buf[k, i, :n])
        g = g_index(modes[k])
        c_buf[k, g, :n] = fold(total)
        for j in range(1, NG):
            mine_ref = c_buf.at[k, g, pl.ds(0, n)]
            pltpu.make_async_remote_copy(
                src_ref=mine_ref, dst_ref=mine_ref,
                send_sem=c_send.at[k], recv_sem=c_recv.at[k],
                device_id=g_peer(modes[k], j)[1], device_id_type=MESH,
            ).start()

    odd = lax.rem(w, 2)
    unit_blocks = [w, w + 2 * odd - 1, w + 2 - 4 * odd, w + 4]

    def unit_lanes(k):
        unit = lax.div(lax.rem(unit_blocks[k] + NZ, NZ), 2)
        return pl.ds(pl.multiple_of(unit * 128, 128), 128)

    def stage_d(k):
        n = len(groups[k])
        wait_bytes(c_buf.at[k, pl.ds(0, NG - 1), pl.ds(0, n)], c_recv.at[k])
        for s, shift in enumerate(groups[k]):
            gh_s[block_rows(shift), :] = unfold(c_buf[k, :, s])
        if k > 0:
            pair = unit_lanes(k - 1)
            gh_out[:, pair] = jnp.transpose(gh_s[pair, :])[:COLS, :]

    GB = 256

    def rows_grad(b):
        cols = pl.ds(pl.multiple_of(b * GB, GB), GB)
        dquant = jnp.dot(ht_s[:COLS, :], dl_s[:, cols], preferred_element_type=f32)
        usable = (fl1[:, cols] == 0).astype(f32)
        ratios = w_v[:, cols] * (1.0 / sc1[:, cols])
        rounded = jnp.floor(ratios + 0.5)
        levels = jnp.clip(rounded, -8.0, 7.0)
        inside = (rounded == levels).astype(f32)
        gw_out[:, cols] = inside * dquant + (DECAY * usable) * w_v[:, cols]
        terms = jnp.sum(dquant * (levels - inside * ratios), axis=0, keepdims=True)
        for i in range(GB // 128):
            f_buf[w, pl.ds(b * (GB // 128) + i, 1), :] = terms[:, i * 128 : (i + 1) * 128]

    @pl.loop(0, 3)
    def _(step):
        ag_step(step)

        @pl.loop(0, 2)
        def _(side):
            form_squares((step + 1) * (2 * side - 1))

        @pl.when(step == 0)
        def _():
            wait_bytes(st_a.at[pl.ds(0, NG - 1)], sa_recv)
            best, weight, pick = merge(st_a, NG)
            st_b[y] = jnp.concatenate([best, weight, pick, jnp.zeros((5, 128), f32)], axis=0)
            for j in range(1, NY):
                pltpu.make_async_remote_copy(
                    src_ref=st_b.at[y], dst_ref=st_b.at[y], send_sem=sb_send, recv_sem=sb_recv,
                    device_id=y_peer("x", j)[1], device_id_type=MESH,
                ).start()

        @pl.when(step == 1)
        def _():
            wait_bytes(st_b.at[pl.ds(0, NY - 1)], sb_recv)
            best, weight, pick = merge(st_b, NY)
            lane_row = lax.broadcasted_iota(i32, (1, 128), 1)
            loss_row = jnp.where(lane_row < TB, best + jnp.log(weight) - pick, 0.0)
            f_buf[w, pl.ds(8, 8), :] = jnp.broadcast_to(loss_row, (8, 128))
            factor = jnp.exp(st_a[g, 0:1, :] - best) / weight
            factor = factor * (1.0 / (ROOT_TOP * ROOT_TOP))
            st_z[w] = jnp.broadcast_to(factor, (8, 128))
            for j in range(1, NZ):
                pltpu.make_async_remote_copy(
                    src_ref=st_z.at[w], dst_ref=st_z.at[w], send_sem=sz_send, recv_sem=sz_recv,
                    device_id=z_peer(j), device_id_type=MESH,
                ).start()
            zt_s[...] = jnp.transpose(jnp.broadcast_to(factor, (128, 128)))
            form_squares(0)
            stage_a(0)

    wait_bytes(st_z.at[pl.ds(0, NZ - 1)], sz_recv)
    rows_of = [st_z[i, 0:1, :] for i in range(NZ)]
    zt_s[...] = jnp.transpose(
        jnp.concatenate(rows_of + [jnp.zeros((120, 128), f32)], axis=0)
    )

    stage_a(2)
    stage_a(1)
    stage_a(3)
    stage_b(0)
    ag_last()
    form_squares(4)
    stage_a(4)

    @pl.loop(0, 2)
    def _(b):
        rows_grad(b)

    stage_b(2)
    stage_b(1)
    stage_c(0)
    stage_b(3)
    stage_b(4)

    @pl.loop(2, 4)
    def _(b):
        rows_grad(b)

    for j in range(1, NZ):
        pltpu.make_async_remote_copy(
            src_ref=f_buf.at[w], dst_ref=f_buf.at[w], send_sem=f_send, recv_sem=f_recv,
            device_id=z_peer(j), device_id_type=MESH,
        ).start()
    stage_c(2)
    stage_c(1)
    stage_c(3)
    stage_c(4)
    wait_bytes(f_buf.at[pl.ds(0, NZ - 1)], f_recv)
    tail = f_buf[0]
    for i in range(1, NZ):
        tail += f_buf[i]
    gs_out[...] = tail[:8, :] * (1.0 / math.sqrt(D * 7.0))
    loss_out[...] = jnp.sum(tail[8:9, :], axis=1, keepdims=True)
    end_copies = [
        pltpu.make_async_copy(gs_out, gs_hbm, end_sem.at[0]),
        pltpu.make_async_copy(loss_out, loss_hbm, end_sem.at[1]),
    ]
    for copy in end_copies:
        copy.start()
    stage_d(0)
    stage_d(1)
    stage_d(2)
    stage_d(3)
    stage_d(4)

    for copy in end_copies:
        copy.wait()
    for k in range(len(groups)):
        n = len(groups[k])
        wait_bytes(a_out.at[k, pl.ds(0, NG - 1), pl.ds(0, n)], a_send.at[k])
        wait_bytes(b_buf.at[k, pl.ds(0, NY - 1), pl.ds(0, n)], b_send.at[k])
        wait_bytes(c_buf.at[k, pl.ds(0, NG - 1), pl.ds(0, n)], c_send.at[k])
    wait_bytes(st_a.at[pl.ds(0, NG - 1)], sa_send)
    wait_bytes(st_b.at[pl.ds(0, NY - 1)], sb_send)
    wait_bytes(st_z.at[pl.ds(0, NZ - 1)], sz_send)
    wait_bytes(f_buf.at[pl.ds(0, NZ - 1)], f_send)
    for way in (0, 1):
        for step in range(4):
            for sub in range(NS):
                if step > 0 or sub in firsts[way]:
                    rs_copy(way, step, sub).wait_send()
                if step < 3 or sub in firsts[way]:
                    ag_copy(way, step, sub).wait_send()


def per_device(hidden, weight, scale, flags, targets):
    f32, bf16, i16 = jnp.float32, jnp.bfloat16, jnp.int16
    vmem = pl.BlockSpec(memory_space=pltpu.VMEM)
    anywhere = pl.BlockSpec(memory_space=pl.ANY)
    dma = pltpu.SemaphoreType.DMA
    grad_weight, grad_scale, grad_hidden, loss = pl.pallas_call(
        kernel,
        out_shape=(
            pltpu.VMEM((COLS, ROWS), f32),
            jax.ShapeDtypeStruct((8, 128), f32),
            pltpu.VMEM((COLS, 512), f32),
            jax.ShapeDtypeStruct((1, 1), f32),
        ),
        in_specs=[anywhere] * 5,
        out_specs=(vmem, anywhere, vmem, anywhere),
        scratch_shapes=[
            pltpu.VMEM((8, 128), f32),
            pltpu.VMEM((1, 1), f32),
            pltpu.VMEM((COLS, ROWS), f32),
            pltpu.VMEM((1, ROWS), f32),
            pltpu.VMEM((1, ROWS), jnp.int32),
            pltpu.VMEM((4, 128), jnp.int32),
            pltpu.VMEM((PAD, 512), bf16),
            pltpu.VMEM((PAD, ROWS), bf16),
            pltpu.VMEM((512, PAD), bf16),
            pltpu.VMEM((512, ROWS), f32),
            pltpu.VMEM((512, ROWS), bf16),
            pltpu.VMEM((128, 128), f32),
            pltpu.VMEM((128, 128), f32),
            pltpu.VMEM((TB, 128), f32),
            pltpu.VMEM((TB, ROWS), f32),
            pltpu.VMEM((2, 4, NS, HB, ROWS + 128), i16),
            pltpu.VMEM((2, 4, NS, HB, ROWS + 128), i16),
            pltpu.VMEM((NZ, NS, HB, ROWS), i16),
            pltpu.VMEM((NG, 8, 128), f32),
            pltpu.VMEM((NY, 8, 128), f32),
            pltpu.VMEM((NZ, 8, 128), f32),
            pltpu.VMEM((512, PAD), f32),
            pltpu.VMEM((5, NG, 2, 16, FOLD), i16),
            pltpu.VMEM((5, NG, 2, 16, FOLD), i16),
            pltpu.VMEM((5, NY, 2, 16, FOLD), i16),
            pltpu.VMEM((5, NG, 2, 16, FOLD), i16),
            pltpu.VMEM((NZ, 16, 128), f32),
            dma((4,)),
            dma(()),
            dma((3,)),
            dma((2,)),
            dma((2, 4, NS)),
            dma((2, 4, NS)),
            dma((2, 4, NS)),
            dma((2, 4, NS)),
            dma(()),
            dma(()),
            dma(()),
            dma(()),
            dma(()),
            dma(()),
            dma((5,)),
            dma((5,)),
            dma((5,)),
            dma((5,)),
            dma((5,)),
            dma((5,)),
            dma(()),
            dma(()),
        ],
        compiler_params=pltpu.CompilerParams(
            collective_id=0, has_side_effects=True, vmem_limit_bytes=58 * 1024 * 1024
        ),
    )(
        hidden.T,
        weight.T,
        scale.reshape(1, ROWS),
        flags.reshape(1, ROWS),
        targets.reshape(4, 128),
    )
    return (grad_weight.T, grad_scale.reshape(ROWS), grad_hidden.T, loss.reshape(()))


def solution(mesh):
    placed = (P(None, "width"), P("vocab", "width"), P("vocab"), P("vocab"), P())
    return jax.shard_map(
        per_device,
        mesh=mesh,
        in_specs=placed,
        out_specs=(P("vocab", "width"), P("vocab"), P(None, "width"), P()),
        check_vma=False,
    )
```

```python
import functools
import math

import jax
import jax.numpy as jnp
from jax import lax
from jax.experimental import pallas as pl
from jax.experimental.pallas import tpu as pltpu
from jax.sharding import PartitionSpec as P

D = 5376
NEG_FILL = -1e30
DECAY = 0.1
MESH = pl.DeviceIdType.MESH

NZ = 8
NG = 8
NY = 4
TB = 64
NS = 4
HB = TB // NS
ROWS = 1024
COLS = 672
PAD = 768
FOLD = 384

CODE_TOP = 32000.0
UNIT = math.log(2.0) / 256.0
ROOT_TOP = 65535.0
ROOT_MID = 32768.0


def code_step(x, top_code, axis):
    top = jnp.max(jnp.abs(x), axis=axis, keepdims=True)
    e = jnp.ceil(jnp.log(jnp.maximum(top, 1e-30) * (1.0 / top_code)) * (1.0 / UNIT))
    return e, jnp.exp(e * (-UNIT))


def to_codes(x, inv):
    return jnp.floor(x * inv + 0.5)


def kernel(
    hid_hbm, w_hbm, sc_hbm, fl_hbm, tg_hbm,
    gw_out, gs_hbm, gh_out, loss_hbm,
    gs_out, loss_out, w_v, sc1, fl1, tg4, ht_s, q_s, h_s, part, dl_s, tr_s, zt_s, own_s, root_s,
    rs_out, rs_in, ag_s, st_a, st_b, st_z, gh_s, a_out, a_in, b_buf, c_buf, f_buf,
    w_sem, h_sem, small_sem, end_sem,
    rs_send, rs_recv, ag_send, ag_recv,
    sa_send, sa_recv, sb_send, sb_recv, sz_send, sz_recv,
    a_send, a_recv, b_send, b_recv, c_send, c_recv, f_send, f_recv,
):
    f32, bf16, i32, i16 = jnp.float32, jnp.bfloat16, jnp.int32, jnp.int16
    v = lax.axis_index("vocab")
    w = lax.axis_index("width")
    core = lax.rem(v, 2)
    x = lax.rem(lax.div(v, 2), 4)
    y = lax.div(v, 8)
    right = (v, lax.rem(w + 1, NZ))
    left = (v, lax.rem(w + NZ - 1, NZ))

    def g_index(mode):
        return (x if mode == "x" else y) * 2 + core

    def g_peer(mode, j):
        other = lax.rem(g_index(mode) + j, NG)
        far, far_core = lax.div(other, 2), lax.rem(other, 2)
        if mode == "x":
            return other, ((y * 4 + far) * 2 + far_core, w)
        return other, ((far * 4 + x) * 2 + far_core, w)

    def y_index(mode):
        return y if mode == "x" else x

    def y_peer(mode, j):
        other = lax.rem(y_index(mode) + j, NY)
        if mode == "x":
            return other, ((other * 4 + x) * 2 + core, w)
        return other, ((y * 4 + other) * 2 + core, w)

    def z_peer(j):
        return (v, lax.rem(w + j, NZ))

    def block_rows(shift, half=None):
        block = lax.rem(w + (shift + 2 * NZ), NZ)
        if half is None:
            return pl.ds(pl.multiple_of(block * TB, TB), TB)
        return pl.ds(pl.multiple_of(block * TB + half * HB, HB), HB)

    small_copies = [
        pltpu.make_async_copy(src, dst, small_sem.at[i])
        for i, (src, dst) in enumerate([(tg_hbm, tg4), (sc_hbm, sc1), (fl_hbm, fl1)])
    ]
    for copy in small_copies:
        copy.start()
    WB = 256

    def w_copy(i):
        cols = pl.ds(pl.multiple_of(i * WB, WB), WB)
        return pltpu.make_async_copy(w_hbm.at[:, cols], w_v.at[:, cols], w_sem.at[i])

    @pl.loop(0, ROWS // WB)
    def _(i):
        w_copy(i).start()

    h_copy = pltpu.make_async_copy(hid_hbm, ht_s.at[pl.ds(0, COLS)], h_sem)
    h_copy.start()

    barrier = pltpu.get_barrier_semaphore()
    for j in range(1, NZ):
        pl.semaphore_signal(barrier, inc=1, device_id=z_peer(j), device_id_type=MESH)
    for j in range(1, NG):
        pl.semaphore_signal(
            barrier, inc=1, device_id=g_peer("x", j)[1], device_id_type=MESH
        )
    for j in range(2, NG):
        far = lax.rem(y + lax.div(j, 2), 4)
        pl.semaphore_signal(
            barrier,
            inc=1,
            device_id=((far * 4 + x) * 2 + j % 2, w),
            device_id_type=MESH,
        )

    for copy in small_copies:
        copy.wait()
    tr_s[...] = jnp.transpose(
        jnp.concatenate([tg4[...].astype(f32), jnp.zeros((124, 128), f32)], axis=0)
    )
    ht_s[COLS:, :] = jnp.zeros((PAD - COLS, 512), bf16)
    q_s[COLS:, :] = jnp.zeros((PAD - COLS, ROWS), bf16)
    h_copy.wait()

    @pl.loop(0, ROWS // WB)
    def _(i):
        w_copy(i).wait()
        tokens = pl.ds(pl.multiple_of(i * 128, 128), 128)
        h_s[tokens, :] = jnp.transpose(ht_s[:, tokens])
        cols = pl.ds(pl.multiple_of(i * WB, WB), WB)
        scale = sc1[:, cols]
        rounded = jnp.floor(w_v[:, cols] * (1.0 / scale) + 0.5)
        levels = jnp.clip(rounded, -8.0, 7.0)
        q_s[:COLS, cols] = (scale * levels).astype(bf16)

    def logits_of(shifts):
        rows = [h_s[block_rows(shift), :] for shift in shifts]
        values = jnp.dot(
            jnp.concatenate(rows, axis=0) if len(shifts) > 1 else rows[0],
            q_s[...],
            preferred_element_type=f32,
        )
        for i, shift in enumerate(shifts):
            part[block_rows(shift), :] = values[i * TB : (i + 1) * TB, :]

    logits_of((4,))
    pl.semaphore_wait(barrier, (NZ - 1) + (NG - 1) + (NG - 2))

    lane_half = lax.broadcasted_iota(i32, (HB, 128), 1)

    def rs_copy(way, step, half):
        return pltpu.make_async_remote_copy(
            src_ref=rs_out.at[way, step, half],
            dst_ref=rs_in.at[way, step, half],
            send_sem=rs_send.at[way, step, half],
            recv_sem=rs_recv.at[way, step, half],
            device_id=right if way == 0 else left,
            device_id_type=MESH,
        )

    def encode(value, ref):
        e, inv = code_step(value, 4.0 * CODE_TOP, 1)
        codes = to_codes(value, inv).astype(i32)
        ref[:, :ROWS] = (codes >> 2).astype(i16)
        low = codes & 3
        pairs = low[:, :128]
        for i in range(1, ROWS // 128):
            pairs = pairs | (low[:, i * 128 : (i + 1) * 128] << (2 * i))
        ref[:, ROWS:] = jnp.where(lane_half == 0, e.astype(i32), pairs).astype(i16)

    def decode(ref):
        high = ref[:, :ROWS].astype(i32) << 2
        pairs = ref[:, ROWS:].astype(i32)
        unit = jnp.exp(pairs[:, :1].astype(f32) * UNIT)
        blocks = []
        for i in range(ROWS // 128):
            low = jnp.where(lane_half == 0, 1.5, ((pairs >> (2 * i)) & 3).astype(f32))
            blocks.append(high[:, i * 128 : (i + 1) * 128].astype(f32) + low)
        return jnp.concatenate(blocks, axis=1) * unit

    def rs_get(way, step, sub):
        return decode(rs_in.at[way, step, sub])

    def mine(shift, half):
        return part[block_rows(shift, half), :]

    firsts = ([s for s in range(NS) if s < NS // 2], [s for s in range(NS) if s >= NS // 2])

    def rs_pair(n, add):
        step = lax.div(n, NS)
        subs = (lax.rem(n + NS // 2, NS), lax.rem(n, NS))
        if add:
            for way in (0, 1):
                rs_copy(way, step - 1, subs[way]).wait_recv()
        values = [mine(4 - step, subs[0]), mine(step - 4, subs[1])]
        if add:
            values = [values[way] + rs_get(way, step - 1, subs[way]) for way in (0, 1)]
        for way in (0, 1):
            encode(values[way], rs_out.at[way, step, subs[way]])
        for way in (0, 1):
            rs_copy(way, step, subs[way]).start()

    @pl.loop(NS // 2, NS)
    def _(n):
        rs_pair(n, False)

    logits_of((3, -3))

    @pl.loop(NS, NS + NS // 2)
    def _(n):
        rs_pair(n, False)

    logits_of((2, -2))

    @pl.loop(NS + NS // 2, 2 * NS)
    def _(n):
        rs_pair(n, True)

    logits_of((1, -1, 0))

    @pl.loop(2 * NS, 4 * NS)
    def _(n):
        rs_pair(n, True)

    def ag_ref(way, step, sub):
        block = lax.rem(w + (step if way == 1 else NZ - step), NZ)
        return ag_s.at[block, sub]

    def ag_copy(way, step, sub):
        ref = ag_ref(way, step, sub)
        return pltpu.make_async_remote_copy(
            src_ref=ref,
            dst_ref=ref,
            send_sem=ag_send.at[way, step, sub],
            recv_sem=ag_recv.at[way, step, sub],
            device_id=right if way == 0 else left,
            device_id_type=MESH,
        )

    def ag_wait(way, step, sub):
        ref = ag_ref(way, step + 1, sub)
        pltpu.make_async_copy(ref, ref, ag_recv.at[way, step, sub]).wait()

    def ag_step(step):
        for sub in range(NS):
            for way in (0, 1):
                ag_wait(way, step, sub)
                if sub in firsts[way]:
                    ag_copy(way, step + 1, sub).start()
                else:

                    @pl.when(step < 2)
                    def _():
                        ag_copy(way, step + 1, sub).start()

    def ag_last():
        for way in (0, 1):
            for sub in firsts[way]:
                ag_wait(way, 3, sub)

    usable_row = fl1[...] == 0

    def pick_lane(ref, index, rows):
        at = lax.broadcasted_iota(i32, (rows.size, 128), 1)
        return jnp.sum(jnp.where(at == index, ref[rows, :], 0.0), axis=1, keepdims=True)

    def hits(block, first, count):
        rows = pl.ds(pl.multiple_of(lax.rem(block, 2) * TB + first, count), count)
        column = pick_lane(tr_s, lax.div(block, 2), rows).astype(i32) - v * ROWS
        return lax.broadcasted_iota(i32, (count, ROWS), 1) == column

    @pl.loop(0, NS)
    def _(sub):
        for way in (0, 1):
            rs_copy(way, 3, sub).wait_recv()
        own = mine(0, sub) + rs_get(0, 3, sub) + rs_get(1, 3, sub)
        masked = jnp.where(usable_row, own, NEG_FILL)
        top = jnp.max(masked, axis=1, keepdims=True)
        root = jnp.where(usable_row, jnp.exp((masked - top) * 0.5), 0.0)
        codes = jnp.floor(root * ROOT_TOP + (0.5 - ROOT_MID))
        ag_s[w, sub] = codes.astype(i32).astype(i16)
        for way in (0, 1):
            ag_copy(way, 0, sub).start()
        rows = pl.ds(pl.multiple_of(sub * HB, HB), HB)
        part[block_rows(0, sub), :] = own
        root_s[rows, :] = root
        own_s[rows, :] = jnp.broadcast_to(top, (HB, 128))

    lane = lax.broadcasted_iota(i32, (TB, 128), 1)
    total = jnp.sum(root_s[...] * root_s[...], axis=1, keepdims=True)
    picked = jnp.sum(
        jnp.where(hits(w, 0, TB), part[block_rows(0), :], 0.0), axis=1, keepdims=True
    )
    stats = jnp.where(
        lane == 0,
        own_s[...],
        jnp.where(lane == 1, total, jnp.where(lane == 2, picked, 0.0)),
    )

    stats = jnp.transpose(jnp.concatenate([stats, jnp.zeros((TB, 128), f32)], axis=0))
    g = g_index("x")
    st_a[g] = stats[:8, :]
    for j in range(1, NG):
        pltpu.make_async_remote_copy(
            src_ref=st_a.at[g], dst_ref=st_a.at[g], send_sem=sa_send, recv_sem=sa_recv,
            device_id=g_peer("x", j)[1], device_id_type=MESH,
        ).start()

    def wait_bytes(ref, sem):
        pltpu.make_async_copy(ref, ref, sem).wait()

    def merge(buf, n):
        best = buf[0, 0:1, :]
        for i in range(1, n):
            best = jnp.maximum(best, buf[i, 0:1, :])
        weight = jnp.zeros((1, 128), f32)
        pick = jnp.zeros((1, 128), f32)
        for i in range(n):
            weight += buf[i, 1:2, :] * jnp.exp(buf[i, 0:1, :] - best)
            pick += buf[i, 2:3, :]
        return best, weight, pick

    def form_dlogits(shift):
        block = lax.rem(w + (shift + NZ), NZ)
        factor = pick_lane(zt_s, block, pl.ds(0, TB))
        dl_s[block_rows(shift), :] = (
            part[block_rows(shift), :] * factor - hits(block, 0, TB).astype(f32)
        ).astype(bf16)

    def form_squares(shift):
        block = lax.rem(w + (shift + NZ), NZ)
        codes = jnp.concatenate([ag_s[block, s] for s in range(NS)], axis=0)
        root = codes.astype(i32).astype(f32) + ROOT_MID
        part[block_rows(shift), :] = root * root

    groups = [(0,), (-1, 1), (-3, -2, 2, 3), (4,)]
    modes = ["x", "x", "y", "x"]
    units = [(), (0,), (1, 2), (3,)]
    nt = (((1,), (1,)), ((), ()))

    def fold(x):
        n = x.shape[0] // 8
        e, inv = code_step(x, CODE_TOP, 1)
        wide = lax.broadcasted_iota(i32, (8 * n, PAD), 1)
        codes = jnp.where(wide < COLS, to_codes(x, inv), e).astype(i32)
        return jnp.concatenate(
            [codes[:, :FOLD].reshape(n, 8, FOLD), codes[:, FOLD:].reshape(n, 8, FOLD)], axis=1
        ).astype(i16)

    def unfold(piece):
        n = piece.shape[0]
        codes = piece.astype(i32).astype(f32)
        low = codes[:, :8, :].reshape(8 * n, FOLD)
        high = codes[:, 8:, :].reshape(8 * n, FOLD)
        unit = jnp.exp(high[:, FOLD - 1 :] * UNIT)
        wide = jnp.concatenate([low, high], axis=1)
        lane_pad = lax.broadcasted_iota(i32, (8 * n, PAD), 1)
        return jnp.where(lane_pad < COLS, wide * unit, 0.0)

    def stage_a(k):
        n = len(groups[k])
        for shift in groups[k]:
            form_dlogits(shift)
        terms = [dl_s[block_rows(shift), :] for shift in groups[k]]
        term = lax.dot_general(
            jnp.concatenate(terms, axis=0) if n > 1 else terms[0],
            q_s[...],
            nt,
            preferred_element_type=f32,
        )
        g = g_index(modes[k])
        for s in range(n):
            a_out[k, :, s] = fold(term[s * TB : (s + 1) * TB])
        a_in[k, g] = a_out[k, g]
        for j in range(1, NG):
            other, device = g_peer(modes[k], j)
            pltpu.make_async_remote_copy(
                src_ref=a_out.at[k, other, pl.ds(0, n)], dst_ref=a_in.at[k, g, pl.ds(0, n)],
                send_sem=a_send.at[k], recv_sem=a_recv.at[k],
                device_id=device, device_id_type=MESH,
            ).start()

    def stage_b(k):
        n = len(groups[k])
        wait_bytes(a_in.at[k, pl.ds(0, NG - 1), pl.ds(0, n)], a_recv.at[k])
        total = unfold(a_in[k, 0, :n])
        for i in range(1, NG):
            total += unfold(a_in[k, i, :n])
        at = y_index(modes[k])
        b_buf[k, at, :n] = fold(total)
        for j in range(1, NY):
            mine_ref = b_buf.at[k, at, pl.ds(0, n)]
            pltpu.make_async_remote_copy(
                src_ref=mine_ref, dst_ref=mine_ref,
                send_sem=b_send.at[k], recv_sem=b_recv.at[k],
                device_id=y_peer(modes[k], j)[1], device_id_type=MESH,
            ).start()

    def stage_c(k):
        n = len(groups[k])
        wait_bytes(b_buf.at[k, pl.ds(0, NY - 1), pl.ds(0, n)], b_recv.at[k])
        total = unfold(b_buf[k, 0, :n])
        for i in range(1, NY):
            total += unfold(b_buf[k, i, :n])
        g = g_index(modes[k])
        c_buf[k, g, :n] = fold(total)
        for j in range(1, NG):
            mine_ref = c_buf.at[k, g, pl.ds(0, n)]
            pltpu.make_async_remote_copy(
                src_ref=mine_ref, dst_ref=mine_ref,
                send_sem=c_send.at[k], recv_sem=c_recv.at[k],
                device_id=g_peer(modes[k], j)[1], device_id_type=MESH,
            ).start()

    odd = lax.rem(w, 2)
    unit_blocks = [w, w + 2 * odd - 1, w + 2 - 4 * odd, w + 4]

    def unit_lanes(k):
        unit = lax.div(lax.rem(unit_blocks[k] + NZ, NZ), 2)
        return pl.ds(pl.multiple_of(unit * 128, 128), 128)

    def stage_d(k):
        n = len(groups[k])
        wait_bytes(c_buf.at[k, pl.ds(0, NG - 1), pl.ds(0, n)], c_recv.at[k])
        for s, shift in enumerate(groups[k]):
            gh_s[block_rows(shift), :] = unfold(c_buf[k, :, s])
        for i in units[k]:
            pair = unit_lanes(i)
            gh_out[:, pair] = jnp.transpose(gh_s[pair, :])[:COLS, :]

    GB = 256

    def rows_grad(b):
        cols = pl.ds(pl.multiple_of(b * GB, GB), GB)
        dquant = jnp.dot(ht_s[:COLS, :], dl_s[:, cols], preferred_element_type=f32)
        usable = (fl1[:, cols] == 0).astype(f32)
        ratios = w_v[:, cols] * (1.0 / sc1[:, cols])
        rounded = jnp.floor(ratios + 0.5)
        levels = jnp.clip(rounded, -8.0, 7.0)
        inside = (rounded == levels).astype(f32)
        gw_out[:, cols] = inside * dquant + (DECAY * usable) * w_v[:, cols]
        terms = jnp.sum(dquant * (levels - inside * ratios), axis=0, keepdims=True)
        for i in range(GB // 128):
            f_buf[w, pl.ds(b * (GB // 128) + i, 1), :] = terms[:, i * 128 : (i + 1) * 128]

    @pl.loop(0, 3)
    def _(step):
        ag_step(step)

        @pl.loop(0, 2)
        def _(side):
            form_squares((step + 1) * (2 * side - 1))

        @pl.when(step == 0)
        def _():
            wait_bytes(st_a.at[pl.ds(0, NG - 1)], sa_recv)
            best, weight, pick = merge(st_a, NG)
            st_b[y] = jnp.concatenate([best, weight, pick, jnp.zeros((5, 128), f32)], axis=0)
            for j in range(1, NY):
                pltpu.make_async_remote_copy(
                    src_ref=st_b.at[y], dst_ref=st_b.at[y], send_sem=sb_send, recv_sem=sb_recv,
                    device_id=y_peer("x", j)[1], device_id_type=MESH,
                ).start()

        @pl.when(step == 1)
        def _():
            wait_bytes(st_b.at[pl.ds(0, NY - 1)], sb_recv)
            best, weight, pick = merge(st_b, NY)
            lane_row = lax.broadcasted_iota(i32, (1, 128), 1)
            loss_row = jnp.where(lane_row < TB, best + jnp.log(weight) - pick, 0.0)
            f_buf[w, pl.ds(8, 8), :] = jnp.broadcast_to(loss_row, (8, 128))
            factor = jnp.exp(st_a[g, 0:1, :] - best) / weight
            factor = factor * (1.0 / (ROOT_TOP * ROOT_TOP))
            st_z[w] = jnp.broadcast_to(factor, (8, 128))
            for j in range(1, NZ):
                pltpu.make_async_remote_copy(
                    src_ref=st_z.at[w], dst_ref=st_z.at[w], send_sem=sz_send, recv_sem=sz_recv,
                    device_id=z_peer(j), device_id_type=MESH,
                ).start()
            zt_s[...] = jnp.transpose(jnp.broadcast_to(factor, (128, 128)))
            form_squares(0)
            stage_a(0)

    wait_bytes(st_z.at[pl.ds(0, NZ - 1)], sz_recv)
    rows_of = [st_z[i, 0:1, :] for i in range(NZ)]
    zt_s[...] = jnp.transpose(
        jnp.concatenate(rows_of + [jnp.zeros((120, 128), f32)], axis=0)
    )

    stage_a(2)
    stage_a(1)
    stage_b(0)
    ag_last()
    form_squares(4)
    stage_a(3)

    @pl.loop(0, 2)
    def _(b):
        rows_grad(b)

    stage_b(1)
    stage_c(0)
    stage_b(2)
    stage_b(3)

    @pl.loop(2, 4)
    def _(b):
        rows_grad(b)

    for j in range(1, NZ):
        pltpu.make_async_remote_copy(
            src_ref=f_buf.at[w], dst_ref=f_buf.at[w], send_sem=f_send, recv_sem=f_recv,
            device_id=z_peer(j), device_id_type=MESH,
        ).start()
    stage_c(1)
    stage_c(2)
    stage_c(3)
    wait_bytes(f_buf.at[pl.ds(0, NZ - 1)], f_recv)
    tail = f_buf[0]
    for i in range(1, NZ):
        tail += f_buf[i]
    gs_out[...] = tail[:8, :] * (1.0 / math.sqrt(D * 7.0))
    loss_out[...] = jnp.sum(tail[8:9, :], axis=1, keepdims=True)
    end_copies = [
        pltpu.make_async_copy(gs_out, gs_hbm, end_sem.at[0]),
        pltpu.make_async_copy(loss_out, loss_hbm, end_sem.at[1]),
    ]
    for copy in end_copies:
        copy.start()
    stage_d(0)
    stage_d(1)
    stage_d(2)
    stage_d(3)

    for copy in end_copies:
        copy.wait()
    for k in range(len(groups)):
        n = len(groups[k])
        wait_bytes(a_out.at[k, pl.ds(0, NG - 1), pl.ds(0, n)], a_send.at[k])
        wait_bytes(b_buf.at[k, pl.ds(0, NY - 1), pl.ds(0, n)], b_send.at[k])
        wait_bytes(c_buf.at[k, pl.ds(0, NG - 1), pl.ds(0, n)], c_send.at[k])
    wait_bytes(st_a.at[pl.ds(0, NG - 1)], sa_send)
    wait_bytes(st_b.at[pl.ds(0, NY - 1)], sb_send)
    wait_bytes(st_z.at[pl.ds(0, NZ - 1)], sz_send)
    wait_bytes(f_buf.at[pl.ds(0, NZ - 1)], f_send)
    for way in (0, 1):
        for step in range(4):
            for sub in range(NS):
                if step > 0 or sub in firsts[way]:
                    rs_copy(way, step, sub).wait_send()
                if step < 3 or sub in firsts[way]:
                    ag_copy(way, step, sub).wait_send()


def per_device(hidden, weight, scale, flags, targets):
    f32, bf16, i16 = jnp.float32, jnp.bfloat16, jnp.int16
    vmem = pl.BlockSpec(memory_space=pltpu.VMEM)
    anywhere = pl.BlockSpec(memory_space=pl.ANY)
    dma = pltpu.SemaphoreType.DMA
    grad_weight, grad_scale, grad_hidden, loss = pl.pallas_call(
        kernel,
        out_shape=(
            pltpu.VMEM((COLS, ROWS), f32),
            jax.ShapeDtypeStruct((8, 128), f32),
            pltpu.VMEM((COLS, 512), f32),
            jax.ShapeDtypeStruct((1, 1), f32),
        ),
        in_specs=[anywhere] * 5,
        out_specs=(vmem, anywhere, vmem, anywhere),
        scratch_shapes=[
            pltpu.VMEM((8, 128), f32),
            pltpu.VMEM((1, 1), f32),
            pltpu.VMEM((COLS, ROWS), f32),
            pltpu.VMEM((1, ROWS), f32),
            pltpu.VMEM((1, ROWS), jnp.int32),
            pltpu.VMEM((4, 128), jnp.int32),
            pltpu.VMEM((PAD, 512), bf16),
            pltpu.VMEM((PAD, ROWS), bf16),
            pltpu.VMEM((512, PAD), bf16),
            pltpu.VMEM((512, ROWS), f32),
            pltpu.VMEM((512, ROWS), bf16),
            pltpu.VMEM((128, 128), f32),
            pltpu.VMEM((128, 128), f32),
            pltpu.VMEM((TB, 128), f32),
            pltpu.VMEM((TB, ROWS), f32),
            pltpu.VMEM((2, 4, NS, HB, ROWS + 128), i16),
            pltpu.VMEM((2, 4, NS, HB, ROWS + 128), i16),
            pltpu.VMEM((NZ, NS, HB, ROWS), i16),
            pltpu.VMEM((NG, 8, 128), f32),
            pltpu.VMEM((NY, 8, 128), f32),
            pltpu.VMEM((NZ, 8, 128), f32),
            pltpu.VMEM((512, PAD), f32),
            pltpu.VMEM((4, NG, 4, 16, FOLD), i16),
            pltpu.VMEM((4, NG, 4, 16, FOLD), i16),
            pltpu.VMEM((4, NY, 4, 16, FOLD), i16),
            pltpu.VMEM((4, NG, 4, 16, FOLD), i16),
            pltpu.VMEM((NZ, 16, 128), f32),
            dma((4,)),
            dma(()),
            dma((3,)),
            dma((2,)),
            dma((2, 4, NS)),
            dma((2, 4, NS)),
            dma((2, 4, NS)),
            dma((2, 4, NS)),
            dma(()),
            dma(()),
            dma(()),
            dma(()),
            dma(()),
            dma(()),
            dma((4,)),
            dma((4,)),
            dma((4,)),
            dma((4,)),
            dma((4,)),
            dma((4,)),
            dma(()),
            dma(()),
        ],
        compiler_params=pltpu.CompilerParams(
            collective_id=0, has_side_effects=True, vmem_limit_bytes=58 * 1024 * 1024
        ),
    )(
        hidden.T,
        weight.T,
        scale.reshape(1, ROWS),
        flags.reshape(1, ROWS),
        targets.reshape(4, 128),
    )
    return (grad_weight.T, grad_scale.reshape(ROWS), grad_hidden.T, loss.reshape(()))


def solution(mesh):
    placed = (P(None, "width"), P("vocab", "width"), P("vocab"), P("vocab"), P())
    return jax.shard_map(
        per_device,
        mesh=mesh,
        in_specs=placed,
        out_specs=(P("vocab", "width"), P("vocab"), P(None, "width"), P()),
        check_vma=False,
    )
```
